256 devices in a mesh: dir: 2 (over z_lo), row: 8 (over z_hi, core), col: 16 (over y, x).
Axes of the slice: x: 4, y: 4, z: 8 (z_hi: 4, z_lo: 2; z = z_hi * 2 + z_lo), core: 2. Of those that a mesh axis runs over, the one named last changes fastest.
Arguments:
- prior_y: float32 [2, 12288, 12288], P('dir', 'row', 'col'), as said below
- labels: int32 [12288, 4], replicated, may hold values from 0 to 7
- pivots: int32 [2, 2], replicated, may hold values from 1 to 47, as said below
Outputs:
- schur: float32 [8, 2, 768, 12288], P('row', 'dir', None, 'col')
- lower: float32 [8, 2, 768, 256], P('row', 'dir')
The draws below stay inside these ranges and needn't reach their ends.
Inputs may be any that keep to these rules, and one draw needn't show every extreme that they name: `prior_y`: each direction's matrix is symmetric and positive definite. `pivots`: the two tiles of a direction differ, tile 0 is never named, and all four entries differ.
All inputs are finite; a program needn't handle non-finite values.
Results may differ from the reference program's by a relative error of at most 0.00011.
Values sent between devices are 32-bit elements; how exact they have to be, the bound alone decides.
A program may use at most 128 MiB of HBM per device.

```python
import jax
import jax.numpy as jnp
from jax import lax

CHANNELS = 12288
TILE = 256
N_ROW = 8


def draw_prior_y(key, part):
    key = jax.random.fold_in(key, 11)
    key_basis, key_weight, key_diag = jax.random.split(key, 3)
    modes = CHANNELS // 24
    weights = jax.random.randint(key_weight, (2, modes), 1, 33).astype(jnp.float32) * 0.125
    levels = jax.random.randint(key_basis, (2, CHANNELS, modes), 0, 2)
    basis = (2 * levels - 1).astype(jnp.float32)
    factor = 1.0
    diagonal = jax.random.uniform(key_diag, (2, CHANNELS), jnp.float32, 0.5, 1.5)
    coupled = jnp.einsum('eik,ejk->eij', basis * weights[:, None, :], basis, precision=lax.Precision.HIGHEST)
    coupled = coupled * (factor / modes)
    ids = jnp.arange(CHANNELS)
    on_diag = (ids[:, None] == ids[None, :])[None, :, :]
    return coupled + jnp.where(on_diag, diagonal[:, :, None], 0.0)


def draw_pivots(key, part):
    key = jax.random.fold_in(key, 23)
    key_first, key_step, key_order = jax.random.split(key, 3)
    tiles = CHANNELS // TILE
    first = jax.random.randint(key_first, (), 2, tiles - 1)
    step = jax.random.randint(key_step, (), 1, tiles - 3)
    second = 2 + (first - 2 + step) % (tiles - 3)
    values = jnp.stack([jnp.int32(1), jnp.int32(tiles - 1), first.astype(jnp.int32), second.astype(jnp.int32)])
    order = jax.random.permutation(key_order, 4)
    return values[order].reshape(2, 2).astype(jnp.int32)


def set_ends(values, key, smallest, high):
    dims = values.shape
    place = [jax.random.randint(jax.random.fold_in(key, axis), (), 0, dims[axis]) for axis in range(len(dims))]
    values = values.at[tuple(place)].set(smallest)
    longest = dims.index(max(dims))
    place[longest] = (place[longest] + 1) % dims[longest]
    return values.at[tuple(place)].set(high)


def setup_inputs(seed: int = 0) -> dict:
    splits = jax.random.split(jax.random.key(seed), 4)
    prior_y = draw_prior_y(jax.random.fold_in(splits[3], 71), 0)
    labels = set_ends(jax.random.randint(splits[1], (CHANNELS, 4), 0, 8), jax.random.fold_in(splits[1], 1), 0, 7).astype(jnp.int32)
    pivots = draw_pivots(jax.random.fold_in(splits[3], 71), 0)
    return {"prior_y": prior_y, "labels": labels, "pivots": pivots}


def solve_parts(col_panel, row_panel, pivot):
    factor = jnp.linalg.cholesky(pivot)
    right = jax.scipy.linalg.cho_solve((factor, True), row_panel)
    left = jax.scipy.linalg.cho_solve((factor, True), col_panel.T).T
    inverse = jax.scipy.linalg.cho_solve((factor, True), jnp.eye(TILE, dtype=jnp.float32))
    return (right, left, inverse)

def sweep(matrix, tile_index):
    start = (tile_index * TILE).astype(jnp.int32)
    col_panel = lax.dynamic_slice_in_dim(matrix, start, TILE, 1)
    row_panel = lax.dynamic_slice_in_dim(matrix, start, TILE, 0)
    pivot = lax.dynamic_slice_in_dim(row_panel, start, TILE, 1)
    right, left, inverse = solve_parts(col_panel, row_panel, pivot)
    updated = matrix - jnp.dot(col_panel, right, precision=lax.Precision.HIGHEST)
    zero = jnp.zeros((), jnp.int32)
    updated = lax.dynamic_update_slice(updated, left, (zero, start))
    updated = lax.dynamic_update_slice(updated, right, (start, zero))
    updated = lax.dynamic_update_slice(updated, -inverse, (start, start))
    return updated

def reference(prior_y, labels, pivots):
    quantum = labels.astype(jnp.float32)
    shift = 0.025 * quantum[:, 0] * (quantum[:, 0] + 1.0) + 0.01 * quantum[:, 1] * quantum[:, 1] + 0.01 * quantum[:, 2] * (quantum[:, 2] + 1.0) + 0.005 * quantum[:, 3] * (quantum[:, 3] + 1.0)
    diag_ids = jnp.arange(CHANNELS)
    swept_list = []
    for direction in range(2):
        matrix = prior_y[direction].at[diag_ids, diag_ids].add(shift)
        matrix = sweep(matrix, pivots[direction, 0])
        matrix = sweep(matrix, pivots[direction, 1])
        swept_list.append(matrix)
    match = swept_list[0] + swept_list[1]
    first_cols = match[:, :TILE]
    first_rows = match[:TILE, :]
    factor = jnp.linalg.cholesky(match[:TILE, :TILE])
    lower = jax.scipy.linalg.cho_solve((factor, True), first_cols.T).T
    schur = match - jnp.dot(lower, first_rows, precision=lax.Precision.HIGHEST)
    leading = diag_ids < TILE
    schur = jnp.where(leading[:, None] | leading[None, :], match, schur)
    grouped = (N_ROW, 2, CHANNELS // (2 * N_ROW))
    return (schur.reshape(grouped + (CHANNELS,)), lower.reshape(grouped + (TILE,)))
```

```python
import functools

import jax
import jax.numpy as jnp
from jax import lax
from jax.experimental import pallas as pl
from jax.experimental.pallas import tpu as pltpu
from jax.sharding import PartitionSpec as P

TILE = 256
F32 = jnp.float32
BF16 = jnp.bfloat16
MESH = pl.DeviceIdType.MESH
ROW_BY_COL = ((1,), (0,))
COL_BY_COL = ((0,), (0,))
TREE_ROWS = ((0, 48), (48, 48), (96, 80), (176, 80))
X_PARTS = 2


def dot6(a, b, dims):
    return lax.dot_general(
        a, b, (dims, ((), ())), precision=lax.Precision.HIGHEST, preferred_element_type=F32
    )


def split(x):
    high = x.astype(BF16)
    return high, (x - high.astype(F32)).astype(BF16)


def dot3(a, b, dims):
    ah, al = split(a)
    bh, bl = split(b)

    def one(p, q):
        return lax.dot_general(p, q, (dims, ((), ())), preferred_element_type=F32)

    return one(ah, bh) + (one(ah, bl) + one(al, bh))


def iota(shape, dim):
    return lax.broadcasted_iota(jnp.int32, shape, dim)


def sweep128(block, group=4):
    lanes, subs = iota((8, 128), 1), iota((8, 128), 0)
    width = 8 * group
    hits = [subs == k for k in range(8)]

    def body(_, b):
        s = [b[8 * j : 8 * j + 8, :] for j in range(group)]
        for i in range(group):
            v = [jnp.broadcast_to(s[i][:, 8 * i + m : 8 * i + m + 1], (8, 128)) for m in range(8)]
            for k in range(8):
                vk = v[k]
                inv = 1.0 / vk[k : k + 1, :]
                for j in range(8):
                    if j != k:
                        rj = v[j][k : k + 1, :] * inv
                        v[j] = jnp.where(hits[k], rj, v[j] - vk * rj)
                v[k] = jnp.where(hits[k], -inv, vk * inv)
            inside = (lanes >= 8 * i) & (lanes < 8 * i + 8)
            x = jnp.where(inside, jnp.where(lanes - 8 * i == subs, -1.0, 0.0), s[i])
            r = -v[0] * x[0:1, :]
            for m in range(1, 8):
                r = r - v[m] * x[m : m + 1, :]
            for q in range(1, group):
                j = (i + q) % group
                acc = jnp.where(inside, 0.0, s[j])
                for m in range(8):
                    col = jnp.broadcast_to(s[j][:, 8 * i + m : 8 * i + m + 1], (8, 128))
                    acc = acc - col * r[m : m + 1, :]
                s[j] = acc
            s[i] = r
        r = jnp.concatenate(s, axis=0)
        rest = b[width:, :]
        lane = iota(rest.shape, 1)
        rest = jnp.where(lane < width, 0.0, rest) - dot6(rest[:, :width], r, ROW_BY_COL)
        return pltpu.roll(jnp.concatenate([rest, r], axis=0), 128 - width, 1)

    return lax.fori_loop(0, 128 // width, body, block)


def sweep_step(a_ref, p):
    n = a_ref.shape[0]
    at = pl.multiple_of(p * 128, 128)
    neg = sweep128(a_ref[pl.ds(at, 128), pl.ds(at, 128)])
    x = a_ref[pl.ds(at, 128), :]
    col, row = iota((128, n), 1), iota((128, n), 0)
    x = jnp.where(col // 128 == p, jnp.where(col - at == row, -1.0, 0.0), x)
    r = -dot6(neg, x, ROW_BY_COL)
    a_ref[pl.ds(at, 128), :] = jnp.zeros((128, n), F32)
    a_ref[:, pl.ds(at, 128)] = jnp.zeros((n, 128), F32)
    a_ref[...] = a_ref[...] - dot6(x, r, COL_BY_COL)


def sweep_all(a_ref):
    def step(p, carry):
        sweep_step(a_ref, p)
        return carry

    lax.fori_loop(0, a_ref.shape[0] // 128, step, 0)


def modified(panel, tile, other, col_first):
    ids = col_first + iota(panel.shape, 1)
    local = ids - tile * TILE
    own = (local >= 0) & (local < TILE)
    beside = ids - other * TILE
    gone = (beside >= 0) & (beside < TILE)
    panel = jnp.where(own, jnp.where(local == iota(panel.shape, 0), -1.0, 0.0), panel)
    return jnp.where(gone, 0.0, panel)


def main_kernel(
    cand, pcand, prior, piv,
    raw, x_out, r_out, p0c_out, p0r_out, n_out,
    cm, pm, rs, y, hsib, p2, p2sum, p3, pv, g, u, mparts, pparts,
    sem_p1, sem_c1, s_p2, r_p2, s_p3, r_p3, s_p4, r_p4, s_p5, r_p5,
    s_rs, r_rs, s_h, r_h, s_agr, s_agl, r_ag,
    s_sib, r_sib, s_ga, s_gb, r_g, s_xa, s_xb, r_x, s_raw, r_raw, s_sw, r_sw,
):
    d, r, c = lax.axis_index("dir"), lax.axis_index("row"), lax.axis_index("col")
    s, z_hi = r % 2, r // 2
    z = 2 * z_hi + d
    cx, cy = c % 4, c // 4
    own = s == d

    def at(zz, cc):
        return (zz % 2, 2 * (zz // 2) + s, cc)

    sibling = (d, r + 1 - 2 * s, c)
    partner = (1 - d, r, c)

    def copy(src, dst, send, recv, device):
        return pltpu.make_async_remote_copy(
            src_ref=src, dst_ref=dst, send_sem=send, recv_sem=recv, device_id=device, device_id_type=MESH
        )

    barrier = pltpu.get_barrier_semaphore()
    pl.semaphore_signal(barrier, inc=1, device_id=sibling, device_id_type=MESH)
    for o in range(1, 8):
        pl.semaphore_signal(barrier, inc=1, device_id=at((z + o) % 8, c), device_id_type=MESH)
    for o in range(1, 16):
        pl.semaphore_signal(barrier, inc=1, device_id=at(z, (c + o) % 16), device_id_type=MESH)
    pl.semaphore_wait(barrier, 23)

    def merge_p():
        return copy(pcand, pm, sem_p1.at[0], sem_p1.at[1], sibling)

    def merge_c():
        return copy(cand, cm, sem_c1.at[0], sem_c1.at[1], sibling)

    def p2_copy(o, cc, slot):
        return copy(
            pm.at[pl.ds(pl.multiple_of(32 * cc, 32), 32), :], p2.at[slot], s_p2.at[o - 1], r_p2.at[slot], at(z, cc)
        )

    def rs_copy(o, q, slot):
        return copy(
            cm.at[pl.ds(0, 2), pl.ds(pl.multiple_of(64 * q, 64), 64), :],
            rs.at[slot], s_rs.at[o - 1], r_rs.at[slot], at(2 * q + d, c),
        )

    def h_copy(q):
        rows = pl.ds(pl.multiple_of(64 * q, 64), 64)
        return copy(cm.at[2, rows, :], y.at[2, rows, :], s_h.at[q - 1], r_h.at[0], at(2 * q + d, c))

    def p3_copy(o, q, slot):
        return copy(
            p2sum.at[pl.ds(pl.multiple_of(8 * q, 8), 8), :], p3.at[slot], s_p3.at[o - 1], r_p3.at[slot], at(2 * q + d, c)
        )

    def p4_copy(o, zz, slot):
        rows = pl.ds(pl.multiple_of(32 * c + 8 * slot, 8), 8)
        return copy(pv.at[rows, :], pv.at[rows, :], s_p4.at[o - 1], r_p4.at[slot], at(zz, c))

    def p5_copy(o, cc, slot):
        rows = pl.ds(pl.multiple_of(32 * slot, 32), 32)
        return copy(pv.at[rows, :], pv.at[rows, :], s_p5.at[o - 1], r_p5.at[slot], at(z, cc))

    @pl.when(jnp.logical_not(own))
    def _():
        merge_p().start()
        merge_c().start()

    @pl.when(own)
    def _():
        merge_p().wait_recv()
        pm[...] = pm[...] + pcand[...]
        for o in range(1, 16):
            p2_copy(o, (c + o) % 16, c).start()
        merge_c().wait_recv()
        cm[...] = cm[...] + cand[...]
        for o in range(1, 4):
            rs_copy(o, (z_hi + o) % 4, z_hi).start()

        @pl.when(z_hi == 0)
        def _():
            for q in range(1, 4):
                h_copy(q).start()
            y[2, 0:64, :] = cm[2, 0:64, :]

        total = pm[pl.ds(pl.multiple_of(32 * c, 32), 32), :]
        for o in range(1, 16):
            cc = (c + o) % 16
            p2_copy(o, cc, cc).wait_recv()
            total = total + p2[cc]
        p2sum[...] = total
        for o in range(1, 4):
            p3_copy(o, (z_hi + o) % 4, z_hi).start()
        total = p2sum[pl.ds(pl.multiple_of(8 * z_hi, 8), 8), :]
        for o in range(1, 4):
            q = (z_hi + o) % 4
            p3_copy(o, q, q).wait_recv()
            total = total + p3[q]
        pv[pl.ds(pl.multiple_of(32 * c + 8 * z_hi, 8), 8), :] = total
        for o in range(1, 8):
            p4_copy(o, (z + o) % 8, z_hi).start()
        for o in range(1, 4):
            q = (z_hi + o) % 4
            p4_copy(o, z, q).wait_recv()

    @pl.when(jnp.logical_not(own))
    def _():
        for q in range(4):
            p4_copy(1, z, q).wait_recv()

    for o in range(1, 16):
        p5_copy(o, (c + o) % 16, c).start()

    @pl.when(own)
    def _():
        rows = pl.ds(pl.multiple_of(64 * z_hi, 64), 64)
        total = cm[0:2, rows, :]
        for o in range(1, 4):
            q = (z_hi + o) % 4
            rs_copy(o, q, q).wait_recv()
            total = total + rs[q]
        y[0:2, rows, :] = total

        @pl.when(z_hi != 0)
        def _():
            h_copy(z_hi).wait_recv()

    sign = 1 - 2 * s

    def ag_copy(q, step):
        rows = pl.ds(pl.multiple_of(64 * q, 64), 64)
        send = s_agr if step == 1 else s_agl
        return copy(y.at[:, rows, :], y.at[:, rows, :], send.at[q], r_ag.at[q], at((z + step * sign + 8) % 8, c))

    own_q = z_hi

    def q_at(delta):
        return (((z - sign * delta + 16) % 8 - s) // 2) % 4

    @pl.when(own)
    def _():
        ag_copy(own_q, 1).start()
        ag_copy(own_q, -1).start()
        q2, q6, q4 = q_at(2), q_at(6), q_at(4)
        ag_copy(q2, 1).wait_recv()
        ag_copy(q2, 1).start()
        ag_copy(q6, -1).wait_recv()
        ag_copy(q6, -1).start()
        ag_copy(q4, 1).wait_recv()

    @pl.when(jnp.logical_not(own))
    def _():
        q1, q7, q3, q5 = q_at(1), q_at(7), q_at(3), q_at(5)
        ag_copy(q1, 1).wait_recv()
        ag_copy(q1, 1).start()
        ag_copy(q7, -1).wait_recv()
        ag_copy(q7, -1).start()
        ag_copy(q3, 1).wait_recv()
        ag_copy(q3, 1).start()
        ag_copy(q5, -1).wait_recv()

    def raw_copy(k):
        return copy(
            prior.at[0, pl.ds(pl.multiple_of((1 - d) * 768 + 256 * k, 256), 256), :],
            raw.at[pl.ds(256 * k, 256), :], s_raw.at[k], r_raw.at[k], partner,
        )

    for k in range(3):
        raw_copy(k).start()

    def tree(buf, sends_a, sends_b, recvs, t, p, parts, xs, ys):
        first, count = TREE_ROWS[t]
        count = count // parts
        way = 1 if t % 2 == 0 else -1
        dx = (way * (cx - xs) + 4) % 4
        dy = (way * (cy - ys) + 4) % 4
        depth = dx + dy
        if t < 2:
            to_x = (dy == 0) & (dx < 3)
            to_y = dy < 3
        else:
            to_x = (dy >= 1) & (dx < 3)
            to_y = ((dx == 0) & (dy < 3)) | ((dx >= 1) & (dy == 3))
            depth = depth + jnp.where((dy == 0) & (dx >= 1), 4, 0)
        p = p - depth
        rows = pl.ds(pl.multiple_of(first + (p % parts) * count, 8), count)
        block = buf.at[p // parts, rows, :]
        next_x = at(z, 4 * cy + (cx + way + 4) % 4)
        next_y = at(z, 4 * ((cy + way + 4) % 4) + cx)
        copy_x = copy(block, block, sends_a.at[t, p], recvs.at[t, p], next_x)
        copy_y = copy(block, block, sends_b.at[t, p], recvs.at[t, p], next_y)
        valid = (p >= 0) & (p < buf.shape[0] * parts)
        return valid, depth, to_x, to_y, copy_x, copy_y

    def forward(*args):
        valid, depth, to_x, to_y, copy_x, copy_y = tree(*args)

        @pl.when(valid & (depth > 0))
        def _():
            copy_x.wait_recv()

        @pl.when(valid & to_x)
        def _():
            copy_x.start()

        @pl.when(valid & to_y)
        def _():
            copy_y.start()

    def finish(*args):
        valid, _, to_x, to_y, copy_x, copy_y = tree(*args)

        @pl.when(valid & to_x)
        def _():
            copy_x.wait_send()

        @pl.when(valid & to_y)
        def _():
            copy_y.wait_send()

    k_own = 2 * r + d
    k_sib = 2 * (r + 1 - 2 * s) + d
    xs, ys = k_own % 4, k_own // 4

    def sib_panels(e):
        return copy(y.at[pl.ds(0, 2)], x_out.at[pl.ds(2 * e, 2)], s_sib.at[0], r_sib.at[0], sibling)

    def sib_h():
        return copy(y.at[2], hsib, s_sib.at[1], r_sib.at[1], sibling)

    @pl.when(c == k_sib)
    def _():
        sib_panels(s).start()
        sib_h().start()

    @pl.when(c == 0)
    def _():
        g[...] = y[:, :, 0:TILE]

    g_args = (g, s_ga, s_gb, r_g)

    def g_step(p, carry):
        for t in range(4):
            forward(*g_args, t, p, 1, 0, 0)
        return carry

    lax.fori_loop(0, 3 + 7, g_step, 0)

    @pl.when(c == k_own)
    def _():
        x_out[pl.ds(2 * s, 2)] = y[0:2]
        sib_panels(1 - s).wait_recv()
        sib_h().wait_recv()
        x_out[4] = y[2] + hsib[...]

    x_args = (x_out, s_xa, s_xb, r_x)

    def x_step(p, carry):
        for t in range(4):
            forward(*x_args, t, p, X_PARTS, xs, ys)
        return carry

    lax.fori_loop(0, 5 * X_PARTS + 7, x_step, 0)

    for o in range(1, 16):
        cc = (c + o) % 16
        p5_copy(o, cc, cc).wait_recv()
    for o in range(1, 16):
        p5_copy(o, (c + o) % 16, c).wait_send()

    @pl.when(own)
    def _():
        for o in range(1, 8):
            p4_copy(o, (z + o) % 8, z_hi).wait_send()

    sweep_all(pv)

    gq = g[0:2].reshape(512, TILE)
    us = -dot6(pv[...], gq, ROW_BY_COL)
    u[s] = us
    mparts[s] = g[2] - dot6(gq, us, COL_BY_COL)

    def swap(k, ref, e):
        return copy(ref.at[e], ref.at[e], s_sw.at[k], r_sw.at[k], sibling)

    def swap_r(e):
        return copy(r_out.at[pl.ds(2 * e, 2)], r_out.at[pl.ds(2 * e, 2)], s_sw.at[2], r_sw.at[2], sibling)

    swap(0, u, s).start()
    swap(1, mparts, s).start()

    t0, t1 = piv[s, 0], piv[s, 1]

    def r_step(k, carry):
        cols = pl.ds(pl.multiple_of(k * 256, 256), 256)
        first = c * 768 + k * 256
        ya = modified(y[0, :, cols], t0, t1, first)
        yb = modified(y[1, :, cols], t1, t0, first)
        rk = -dot6(pv[...], jnp.concatenate([ya, yb], axis=0), ROW_BY_COL)
        r_out[2 * s, :, cols] = rk[:TILE]
        r_out[2 * s + 1, :, cols] = rk[TILE:]
        pparts[s, :, cols] = y[2, :, cols] - dot6(gq, rk, COL_BY_COL)
        return carry

    lax.fori_loop(0, 3, r_step, 0)
    swap_r(s).start()
    swap(3, pparts, s).start()

    swap(1, mparts, 1 - s).wait_recv()
    n_out[...] = mparts[0] + mparts[1]
    sweep_all(n_out)

    swap(0, u, 1 - s).wait_recv()

    def p_step(k, carry):
        cols = pl.ds(pl.multiple_of(k * 256, 256), 256)
        first = k_own * 768 + k * 256
        total = x_out[4, :, cols]
        for e in range(2):
            ta, tb = piv[e, 0], piv[e, 1]
            xa = modified(x_out[2 * e, :, cols], ta, tb, first)
            xb = modified(x_out[2 * e + 1, :, cols], tb, ta, first)
            total = total - dot6(u[e], jnp.concatenate([xa, xb], axis=0), COL_BY_COL)
        p0r_out[:, cols] = total
        return carry

    lax.fori_loop(0, 3, p_step, 0)
    swap_r(1 - s).wait_recv()
    swap(3, pparts, 1 - s).wait_recv()
    p0c_out[...] = pparts[0] + pparts[1]

    @pl.when(jnp.logical_not(own))
    def _():
        merge_p().wait_send()
        merge_c().wait_send()
        ag_copy(q_at(1), 1).wait_send()
        ag_copy(q_at(7), -1).wait_send()
        ag_copy(q_at(3), 1).wait_send()

    @pl.when(own)
    def _():
        for o in range(1, 16):
            p2_copy(o, (c + o) % 16, c).wait_send()
        for o in range(1, 4):
            rs_copy(o, (z_hi + o) % 4, z_hi).wait_send()
            p3_copy(o, (z_hi + o) % 4, z_hi).wait_send()

        @pl.when(z_hi == 0)
        def _():
            for q in range(1, 4):
                h_copy(q).wait_send()

        ag_copy(own_q, 1).wait_send()
        ag_copy(own_q, -1).wait_send()
        ag_copy(q_at(2), 1).wait_send()
        ag_copy(q_at(6), -1).wait_send()

    @pl.when(c == k_sib)
    def _():
        sib_panels(s).wait_send()
        sib_h().wait_send()

    def g_end(p, carry):
        for t in range(4):
            finish(*g_args, t, p, 1, 0, 0)
        return carry

    def x_end(p, carry):
        for t in range(4):
            finish(*x_args, t, p, X_PARTS, xs, ys)
        return carry

    lax.fori_loop(0, 3 + 7, g_end, 0)
    lax.fori_loop(0, 5 * X_PARTS + 7, x_end, 0)
    swap(0, u, s).wait_send()
    swap(1, mparts, s).wait_send()
    swap_r(s).wait_send()
    swap(3, pparts, s).wait_send()
    for k in range(3):
        raw_copy(k).wait()


def run_main(cand, pcand, prior, pivots):
    vmem = pl.BlockSpec(memory_space=pltpu.VMEM)
    dma = pltpu.SemaphoreType.DMA
    return pl.pallas_call(
        main_kernel,
        out_shape=(
            jax.ShapeDtypeStruct((768, 768), F32),
            jax.ShapeDtypeStruct((5, 256, 768), F32),
            jax.ShapeDtypeStruct((4, 256, 768), F32),
            jax.ShapeDtypeStruct((256, 768), F32),
            jax.ShapeDtypeStruct((256, 768), F32),
            jax.ShapeDtypeStruct((256, 256), F32),
        ),
        in_specs=[vmem, vmem, pl.BlockSpec(memory_space=pl.ANY), pl.BlockSpec(memory_space=pltpu.SMEM)],
        out_specs=(pl.BlockSpec(memory_space=pl.ANY), vmem, vmem, vmem, vmem, vmem),
        scratch_shapes=[
            pltpu.VMEM((3, 256, 768), F32),
            pltpu.VMEM((512, 512), F32),
            pltpu.VMEM((4, 2, 64, 768), F32),
            pltpu.VMEM((3, 256, 768), F32),
            pltpu.VMEM((256, 768), F32),
            pltpu.VMEM((16, 32, 512), F32),
            pltpu.VMEM((32, 512), F32),
            pltpu.VMEM((4, 8, 512), F32),
            pltpu.VMEM((512, 512), F32),
            pltpu.VMEM((3, 256, 256), F32),
            pltpu.VMEM((2, 512, 256), F32),
            pltpu.VMEM((2, 256, 256), F32),
            pltpu.VMEM((2, 256, 768), F32),
            dma((2,)), dma((2,)),
            dma((15,)), dma((16,)), dma((3,)), dma((4,)), dma((7,)), dma((4,)), dma((15,)), dma((16,)),
            dma((3,)), dma((4,)), dma((3,)), dma((1,)), dma((4,)), dma((4,)), dma((4,)),
            dma((2,)), dma((2,)), dma((4, 3)), dma((4, 3)), dma((4, 3)), dma((4, 5 * X_PARTS)), dma((4, 5 * X_PARTS)), dma((4, 5 * X_PARTS)),
            dma((3,)), dma((3,)), dma((4,)), dma((4,)),
        ],
        compiler_params=pltpu.CompilerParams(
            collective_id=0, has_side_effects=True, vmem_limit_bytes=56 * 1024 * 1024
        ),
    )(cand, pcand, prior, pivots)


def final_kernel(place, piv, own, raw, xt, rr, p0c, p0r, neg, shift, schur, lower):
    step = pl.program_id(0)
    row_first = place[1] * 768 + step * 256
    col_first = place[2] * 768
    rows, cols = row_first + iota((256, 768), 0), col_first + iota((256, 768), 1)
    added = jnp.where(rows == cols, shift[...], 0.0)
    mine = place[0]

    def zeroed(block, e):
        a, b = piv[e, 0], piv[e, 1]
        row_tile, col_tile = rows // TILE, cols // TILE
        hit = (row_tile == a) | (row_tile == b) | (col_tile == a) | (col_tile == b)
        return jnp.where(hit, 0.0, block + added)

    total = zeroed(own[0], mine) + zeroed(raw[...], 1 - mine)
    for e in range(2):
        a, b = piv[e, 0], piv[e, 1]
        xa = modified(xt[2 * e], a, b, row_first)
        xb = modified(xt[2 * e + 1], b, a, row_first)
        x = jnp.concatenate([xa, xb], axis=0)
        y = rr[2 * e : 2 * e + 2].reshape(512, 768)
        total = total - dot3(x, y, COL_BY_COL)
    low = -dot6(p0r[...], neg[...], COL_BY_COL)
    lower[0, 0] = low
    reduced = total - dot3(low, p0c[...], ROW_BY_COL)
    schur[0, 0] = jnp.where((rows < TILE) | (cols < TILE), total, reduced)


def run_final(place, pivots, prior, raw, xt, rr, p0c, p0r, neg, shift):
    whole2 = lambda i, p, v: (0, 0)
    spec = pltpu.PrefetchScalarGridSpec(
        num_scalar_prefetch=2,
        grid=(3,),
        in_specs=[
            pl.BlockSpec((1, 256, 768), lambda i, p, v: (0, 3 * p[0] + i, 0)),
            pl.BlockSpec((256, 768), lambda i, p, v: (i, 0)),
            pl.BlockSpec((5, 256, 256), lambda i, p, v: (0, 0, i)),
            pl.BlockSpec((4, 256, 768), lambda i, p, v: (0, 0, 0)),
            pl.BlockSpec((256, 768), whole2),
            pl.BlockSpec((256, 256), lambda i, p, v: (0, i)),
            pl.BlockSpec((256, 256), whole2),
            pl.BlockSpec((256, 1), lambda i, p, v: (i, 0)),
        ],
        out_specs=(
            pl.BlockSpec((1, 1, 256, 768), lambda i, p, v: (0, 0, i, 0)),
            pl.BlockSpec((1, 1, 256, 256), lambda i, p, v: (0, 0, i, 0)),
        ),
    )
    return pl.pallas_call(
        final_kernel,
        grid_spec=spec,
        out_shape=(
            jax.ShapeDtypeStruct((1, 1, 768, 768), F32),
            jax.ShapeDtypeStruct((1, 1, 768, 256), F32),
        ),
        compiler_params=pltpu.CompilerParams(vmem_limit_bytes=56 * 1024 * 1024),
    )(place, pivots, prior, raw, xt, rr, p0c, p0r, neg, shift)


def shifts(quantum):
    quantum = quantum.astype(F32)
    return (
        0.025 * quantum[:, 0] * (quantum[:, 0] + 1.0)
        + 0.01 * quantum[:, 1] * quantum[:, 1]
        + 0.01 * quantum[:, 2] * (quantum[:, 2] + 1.0)
        + 0.005 * quantum[:, 3] * (quantum[:, 3] + 1.0)
    )


def per_device(prior_y, labels, pivots):
    r, c, d = lax.axis_index("row"), lax.axis_index("col"), lax.axis_index("dir")
    height, width = prior_y.shape[1], prior_y.shape[2]
    row_first, col_first = r * height, c * width
    cols = col_first + jnp.arange(width, dtype=jnp.int32)
    matrix = prior_y[0]

    def tile_rows(tile):
        start = jnp.clip(tile * TILE - row_first, 0, height - TILE)
        block = lax.dynamic_slice_in_dim(matrix, start, TILE, 0)
        shift = shifts(lax.dynamic_slice_in_dim(labels, tile * TILE, TILE, 0))
        ids = tile * TILE + jnp.arange(TILE, dtype=jnp.int32)
        block = block + jnp.where(ids[:, None] == cols[None, :], shift[:, None], 0.0)
        return jnp.where(tile * TILE // height == r, block, 0.0)

    ta, tb = pivots[d, 0], pivots[d, 1]
    first, second, lead = tile_rows(ta), tile_rows(tb), tile_rows(jnp.int32(0))
    gone = (cols // TILE == ta) | (cols // TILE == tb)
    lead = jnp.where(gone[None, :], 0.0, lead)
    cand = jnp.stack([first, second, lead])

    def tile_cols(tile):
        start = jnp.clip(tile * TILE - col_first, 0, width - TILE)
        block = lax.dynamic_slice_in_dim(cand[:2], start, TILE, 2).reshape(2 * TILE, TILE)
        return jnp.where(tile * TILE // width == c, block, 0.0)

    pcand = jnp.concatenate([tile_cols(ta), tile_cols(tb)], axis=1)
    raw, xt, rr, p0c, p0r, neg = run_main(cand, pcand, prior_y, pivots)
    shift = shifts(lax.dynamic_slice_in_dim(labels, row_first + d * 768, 768, 0))[:, None]
    place = jnp.stack([d, 2 * r + d, c]).astype(jnp.int32)
    return run_final(place, pivots, prior_y, raw, xt, rr, p0c, p0r, neg, shift)


def solution(mesh):
    placed = (P("dir", "row", "col"), P(), P())
    return jax.shard_map(
        per_device,
        mesh=mesh,
        in_specs=placed,
        out_specs=(P("row", "dir", None, "col"), P("row", "dir", None, None)),
        check_vma=False,
    )
```

```python
import functools

import jax
import jax.numpy as jnp
from jax import lax
from jax.experimental import pallas as pl
from jax.experimental.pallas import tpu as pltpu
from jax.sharding import PartitionSpec as P

TILE = 256
F32 = jnp.float32
BF16 = jnp.bfloat16
MESH = pl.DeviceIdType.MESH
ROW_BY_COL = ((1,), (0,))
COL_BY_COL = ((0,), (0,))


def dot6(a, b, dims):
    return lax.dot_general(
        a, b, (dims, ((), ())), precision=lax.Precision.HIGHEST, preferred_element_type=F32
    )


def split(x):
    high = x.astype(BF16)
    return high, (x - high.astype(F32)).astype(BF16)


def dot3(a, b, dims):
    ah, al = split(a)
    bh, bl = split(b)

    def one(p, q):
        return lax.dot_general(p, q, (dims, ((), ())), preferred_element_type=F32)

    return one(ah, bh) + (one(ah, bl) + one(al, bh))


def iota(shape, dim):
    return lax.broadcasted_iota(jnp.int32, shape, dim)


def sweep128(block, service, group=4):
    lanes, subs = iota((8, 128), 1), iota((8, 128), 0)
    width = 8 * group
    hits = [subs == k for k in range(8)]

    def body(step, b):
        service(step)
        s = [b[8 * j : 8 * j + 8, :] for j in range(group)]
        for i in range(group):
            v = [jnp.broadcast_to(s[i][:, 8 * i + m : 8 * i + m + 1], (8, 128)) for m in range(8)]
            for k in range(8):
                vk = v[k]
                inv = 1.0 / vk[k : k + 1, :]
                for j in range(8):
                    if j != k:
                        rj = v[j][k : k + 1, :] * inv
                        v[j] = jnp.where(hits[k], rj, v[j] - vk * rj)
                v[k] = jnp.where(hits[k], -inv, vk * inv)
            inside = (lanes >= 8 * i) & (lanes < 8 * i + 8)
            x = jnp.where(inside, jnp.where(lanes - 8 * i == subs, -1.0, 0.0), s[i])
            r = -v[0] * x[0:1, :]
            for m in range(1, 8):
                r = r - v[m] * x[m : m + 1, :]
            for q in range(1, group):
                j = (i + q) % group
                acc = jnp.where(inside, 0.0, s[j])
                for m in range(8):
                    col = jnp.broadcast_to(s[j][:, 8 * i + m : 8 * i + m + 1], (8, 128))
                    acc = acc - col * r[m : m + 1, :]
                s[j] = acc
            s[i] = r
        r = jnp.concatenate(s, axis=0)
        rest = b[width:, :]
        lane = iota(rest.shape, 1)
        rest = jnp.where(lane < width, 0.0, rest) - dot6(rest[:, :width], r, ROW_BY_COL)
        return pltpu.roll(jnp.concatenate([rest, r], axis=0), 128 - width, 1)

    return lax.fori_loop(0, 128 // width, body, block)


def sweep_step(a_ref, p, service):
    n = a_ref.shape[0]
    at = pl.multiple_of(p * 128, 128)
    neg = sweep128(a_ref[pl.ds(at, 128), pl.ds(at, 128)], service)
    x = a_ref[pl.ds(at, 128), :]
    col, row = iota((128, n), 1), iota((128, n), 0)
    x = jnp.where(col // 128 == p, jnp.where(col - at == row, -1.0, 0.0), x)
    r = -dot6(neg, x, ROW_BY_COL)
    a_ref[pl.ds(at, 128), :] = jnp.zeros((128, n), F32)
    a_ref[:, pl.ds(at, 128)] = jnp.zeros((n, 128), F32)
    a_ref[...] = a_ref[...] - dot6(x, r, COL_BY_COL)


def modified(panel, tile, other, col_first):
    ids = col_first + iota(panel.shape, 1)
    local = ids - tile * TILE
    own = (local >= 0) & (local < TILE)
    beside = ids - other * TILE
    gone = (beside >= 0) & (beside < TILE)
    panel = jnp.where(own, jnp.where(local == iota(panel.shape, 0), -1.0, 0.0), panel)
    return jnp.where(gone, 0.0, panel)


def main_kernel(
    a_ref, shift, prior, piv,
    raw, corr, low_out,
    x_buf, r_buf, p0c_buf, n_buf, cand, pcand, cm, pm, rs, y, hpre, p2, p2sum, p3, pv, gr, gsum, gp, g, u, mparts, pparts,
    sem_p1, sem_c1, sem_h1, s_p2, r_p2, s_p3, r_p3, s_p4, r_p4, s_p5, r_p5,
    s_g1, r_g1, s_g2, r_g2, s_g3, r_g3, s_g4, r_g4,
    s_rs, r_rs, s_h, r_h, s_agr, s_agl, r_ag, s_ahr, s_ahl, r_ah,
    s_sib, r_sib, s_sibh, r_sibh, s_xa, s_xb, r_x, s_raw, r_raw, s_sw, r_sw,
):
    d, r, c = lax.axis_index("dir"), lax.axis_index("row"), lax.axis_index("col")
    s, z_hi = r % 2, r // 2
    z = 2 * z_hi + d
    cx, cy = c % 4, c // 4
    own = s == d
    other = s != d

    def at(zz, cc):
        return (zz % 2, 2 * (zz // 2) + s, cc)

    sibling = (d, r + 1 - 2 * s, c)
    partner = (1 - d, r, c)

    def copy(src, dst, send, recv, device):
        return pltpu.make_async_remote_copy(
            src_ref=src, dst_ref=dst, send_sem=send, recv_sem=recv, device_id=device, device_id_type=MESH
        )

    def span(first, count):
        return pl.ds(pl.multiple_of(first, 8), count)

    barrier = pltpu.get_barrier_semaphore()
    pl.semaphore_signal(barrier, inc=1, device_id=sibling, device_id_type=MESH)
    for o in range(1, 8):
        pl.semaphore_signal(barrier, inc=1, device_id=at((z + o) % 8, c), device_id_type=MESH)
    for o in range(1, 16):
        pl.semaphore_signal(barrier, inc=1, device_id=at(z, (c + o) % 16), device_id_type=MESH)

    tiles = (piv[d, 0], piv[d, 1])
    col_ids = c * 768 + iota((TILE, 768), 1)
    for k in range(2):
        named = jnp.full((TILE, 768), tiles[k], jnp.int32)
        block = jnp.zeros((TILE, 768), F32)
        for j in range(6):
            block = jnp.where(named == 6 * r + j, a_ref[0, TILE * j : TILE * j + TILE, :], block)
        ids = tiles[k] * TILE + iota((TILE, 768), 0)
        here = (ids == col_ids) & (ids >= r * 1536) & (ids < r * 1536 + 1536)
        cand[k] = block + jnp.where(here, shift[...], 0.0)
    lead = a_ref[0, 0:TILE, :] + jnp.where(iota((TILE, 768), 0) == col_ids, shift[...], 0.0)
    gone = (col_ids // TILE == tiles[0]) | (col_ids // TILE == tiles[1]) | (iota((TILE, 768), 0) + r * 1536 >= 1536)
    cand[2] = jnp.where(gone, 0.0, lead)
    for k in range(2):
        named = jnp.full((2 * TILE, TILE), tiles[k], jnp.int32)
        block = jnp.zeros((2 * TILE, TILE), F32)
        for j in range(3):
            part = cand[0:2, :, TILE * j : TILE * j + TILE].reshape(2 * TILE, TILE)
            block = jnp.where(named == 3 * c + j, part, block)
        pcand[:, TILE * k : TILE * k + TILE] = block
    pl.semaphore_wait(barrier, 23)

    def merge_p():
        return copy(pcand, pm, sem_p1.at[0], sem_p1.at[1], sibling)

    def merge_c():
        return copy(cand.at[pl.ds(0, 2)], cm.at[pl.ds(0, 2)], sem_c1.at[0], sem_c1.at[1], sibling)

    def h_first():
        return copy(cand.at[2], hpre, sem_h1.at[0], sem_h1.at[1], partner)

    def p2_copy(o, cc, slot):
        return copy(pm.at[span(32 * cc, 32), :], p2.at[slot], s_p2.at[o - 1], r_p2.at[slot], at(z, cc))

    def rs_copy(o, q, slot):
        return copy(
            cm.at[pl.ds(0, 2), span(64 * q, 64), :], rs.at[slot], s_rs.at[o - 1], r_rs.at[slot], at(2 * q + d, c)
        )

    def h_copy(q):
        rows = span(64 * q, 64)
        return copy(cm.at[2, rows, :], y.at[2, rows, :], s_h.at[q - 1], r_h.at[0], at(2 * q + d, c))

    def p3_copy(o, q, slot):
        return copy(p2sum.at[span(8 * q, 8), :], p3.at[slot], s_p3.at[o - 1], r_p3.at[slot], at(2 * q + d, c))

    def p4_copy(o, zz, slot):
        rows = span(32 * c + 8 * slot, 8)
        return copy(pv.at[rows, :], pv.at[rows, :], s_p4.at[o - 1], r_p4.at[slot], at(zz, c))

    def p5_copy(o, cc, slot):
        rows = span(32 * slot, 32)
        return copy(pv.at[rows, :], pv.at[rows, :], s_p5.at[o - 1], r_p5.at[slot], at(z, cc))

    def g1_copy(o, q, slot):
        return copy(
            cm.at[:, span(64 * q, 64), pl.ds(0, TILE)], gr.at[slot], s_g1.at[o - 1], r_g1.at[slot], at(2 * q + d, c)
        )

    def g2_copy(cc):
        return copy(
            gsum.at[:, span(8 * cc, 8), :], gp.at[cc, :, span(8 * z_hi, 8), :], s_g2.at[cc - 1], r_g2.at[0], at(z, cc)
        )

    def g3_copy(o, zz, slot):
        block = gp.at[c, :, span(8 * slot, 8), :]
        return copy(block, block, s_g3.at[o - 1], r_g3.at[slot], at(zz, c))

    def g4_copy(o, cc, slot):
        return copy(gp.at[slot], gp.at[slot], s_g4.at[o - 1], r_g4.at[slot], at(z, cc))

    def raw_copy(k):
        return copy(
            prior.at[0, span((1 - d) * 768 + 256 * k, 256), :],
            raw.at[pl.ds(256 * k, 256), :], s_raw.at[k], r_raw.at[k], partner,
        )

    sends_h = (d == 1) & (r == 0)
    leads_h = (d == 0) & (r == 0)

    @pl.when(other)
    def _():
        merge_p().start()
        merge_c().start()

    @pl.when(sends_h)
    def _():
        h_first().start()

    @pl.when(s == 1)
    def _():
        y[2] = jnp.zeros((TILE, 768), F32)

    def push_g4():
        @pl.when(c < 8)
        def _():
            for o in range(1, 16):
                g4_copy(o, (c + o) % 16, c).start()

    @pl.when(own)
    def _():
        merge_p().wait_recv()
        pm[...] = pm[...] + pcand[...]
        for o in range(1, 16):
            p2_copy(o, (c + o) % 16, c).start()
        merge_c().wait_recv()
        cm[0:2] = cm[0:2] + cand[0:2]

        @pl.when(leads_h)
        def _():
            h_first().wait_recv()
            cm[2] = cand[2] + hpre[...]

        @pl.when(r != d)
        def _():
            cm[2] = jnp.zeros((TILE, 768), F32)

        @pl.when((r == d) & (d == 1))
        def _():
            cm[2] = jnp.zeros((TILE, 768), F32)

        @pl.when(c == 0)
        def _():
            for o in range(1, 4):
                g1_copy(o, (z_hi + o) % 4, z_hi).start()

        for o in range(1, 4):
            rs_copy(o, (z_hi + o) % 4, z_hi).start()

        @pl.when(leads_h)
        def _():
            for q in range(1, 4):
                h_copy(q).start()
            y[2, 0:64, :] = cm[2, 0:64, :]

        total = pm[span(32 * c, 32), :]
        for o in range(1, 16):
            cc = (c + o) % 16
            p2_copy(o, cc, cc).wait_recv()
            total = total + p2[cc]
        p2sum[...] = total
        for o in range(1, 4):
            p3_copy(o, (z_hi + o) % 4, z_hi).start()

        @pl.when(c == 0)
        def _():
            total = cm[:, span(64 * z_hi, 64), 0:TILE]
            for o in range(1, 4):
                q = (z_hi + o) % 4
                g1_copy(o, q, q).wait_recv()
                total = total + gr[q]
            gsum[...] = total
            for cc in range(1, 8):
                g2_copy(cc).start()
            gp[0, :, span(8 * z_hi, 8), :] = total[:, 0:8]

        total = p2sum[span(8 * z_hi, 8), :]
        for o in range(1, 4):
            q = (z_hi + o) % 4
            p3_copy(o, q, q).wait_recv()
            total = total + p3[q]
        pv[span(32 * c + 8 * z_hi, 8), :] = total
        for o in range(1, 8):
            p4_copy(o, (z + o) % 8, z_hi).start()

        @pl.when((c > 0) & (c < 8))
        def _():
            g2_copy(c).wait_recv()

        @pl.when(c < 8)
        def _():
            for o in range(1, 8):
                g3_copy(o, (z + o) % 8, z_hi).start()

        for o in range(1, 4):
            q = (z_hi + o) % 4
            p4_copy(o, z, q).wait_recv()

    @pl.when(other)
    def _():
        for q in range(4):
            p4_copy(1, z, q).wait_recv()

    for o in range(1, 16):
        p5_copy(o, (c + o) % 16, c).start()

    def order(e, k):
        delta = jnp.where(
            e == d,
            jnp.where(k == 0, 0, jnp.where(k == 1, 2, jnp.where(k == 2, 6, 4))),
            jnp.where(k == 0, 1, jnp.where(k == 1, 7, jnp.where(k == 2, 3, 5))),
        )
        return (((z - (1 - 2 * e) * delta + 16) % 8 - e + 8) // 2) % 4

    class Ring:
        def __init__(self, k, step):
            q = order(s, k)
            rows = span(64 * q, 64)
            right = step == 1
            to = at((z + step * (1 - 2 * s) + 8) % 8, c)
            block = y.at[pl.ds(0, 2), rows, :]
            self.main = copy(block, block, (s_agr if right else s_agl).at[q], r_ag.at[q], to)
            block = y.at[2, rows, :]
            self.lead = copy(block, block, (s_ahr if right else s_ahl).at[q], r_ah.at[q], to)

        def both(self, name):
            getattr(self.main, name)()

            @pl.when(s == 0)
            def _():
                getattr(self.lead, name)()

    def arrive(k):
        Ring(k, 1).both("wait_recv")

    def stage(k):
        if k == 0 or k == 2:
            @pl.when(other)
            def _():
                arrive(k)
                Ring(k, 1).both("start")
                arrive(k + 1)
                if k == 0:
                    Ring(k + 1, -1).both("start")
        elif k == 1:
            @pl.when(own)
            def _():
                arrive(1)
                Ring(1, 1).both("start")
                arrive(2)
                Ring(2, -1).both("start")
        else:
            @pl.when(own)
            def _():
                arrive(3)

    @pl.when(own)
    def _():
        rows = span(64 * z_hi, 64)
        total = cm[0:2, rows, :]
        for o in range(1, 4):
            q = (z_hi + o) % 4
            rs_copy(o, q, q).wait_recv()
            total = total + rs[q]
        y[0:2, rows, :] = total

        @pl.when((d == 0) & (r != 0))
        def _():
            h_copy(z_hi).wait_recv()

        Ring(0, 1).both("start")
        Ring(0, -1).both("start")

    k_own = 2 * r + d
    k_sib = 2 * (r + 1 - 2 * s) + d
    xs, ys = k_own % 4, k_own // 4

    def sib_panels(e, k):
        rows = span(64 * order(e, k), 64)
        return copy(
            y.at[pl.ds(0, 2), rows, :], x_buf.at[pl.ds(2 * e, 2), rows, :], s_sib.at[k], r_sib.at[k], sibling
        )

    def sib_h(k):
        rows = span(64 * order(0, k), 64)
        return copy(y.at[2, rows, :], x_buf.at[4, rows, :], s_sibh.at[k], r_sibh.at[k], sibling)

    def to_root(k):
        @pl.when(c == k_sib)
        def _():
            sib_panels(s, k).start()

            @pl.when(s == 0)
            def _():
                sib_h(k).start()

        @pl.when(c == k_own)
        def _():
            rows = span(64 * order(s, k), 64)
            x_buf[pl.ds(2 * s, 2), rows, :] = y[0:2, rows, :]

            @pl.when(s == 0)
            def _():
                x_buf[4, rows, :] = y[2, rows, :]

            sib_panels(1 - s, k).wait_recv()

            @pl.when(s == 1)
            def _():
                sib_h(k).wait_recv()

    def tree(t, slot):
        way = 1 if t % 2 == 0 else -1
        dx = (way * (cx - xs) + 4) % 4
        dy = (way * (cy - ys) + 4) % 4
        depth = dx + dy
        if t < 2:
            to_x = (dy == 0) & (dx < 3)
            to_y = dy < 3
        else:
            to_x = (dy >= 1) & (dx < 3)
            to_y = ((dx == 0) & (dy < 3)) | ((dx >= 1) & (dy == 3))
            depth = depth + jnp.where((dy == 0) & (dx >= 1), 4, 0)
        p = slot - 2 * depth
        valid = (p >= 0) & (p < 20)
        p = jnp.where(valid, p, 0)
        tile = p % 5
        rows = span(64 * order(jnp.where(tile == 4, 0, tile // 2), p // 5) + 16 * t, 16)
        block = x_buf.at[tile, rows, :]
        next_x = at(z, 4 * cy + (cx + way + 4) % 4)
        next_y = at(z, 4 * ((cy + way + 4) % 4) + cx)
        copy_x = copy(block, block, s_xa.at[t, p], r_x.at[t, p], next_x)
        copy_y = copy(block, block, s_xb.at[t, p], r_x.at[t, p], next_y)
        return valid, depth, to_x, to_y, copy_x, copy_y

    def x_slot(slot):
        for t in range(4):
            valid, depth, to_x, to_y, copy_x, copy_y = tree(t, slot)

            @pl.when(valid & (depth > 0))
            def _():
                copy_x.wait_recv()

            @pl.when(valid & to_x)
            def _():
                copy_x.start()

            @pl.when(valid & to_y)
            def _():
                copy_y.start()

    def x_end(slot):
        for t in range(4):
            valid, _, to_x, to_y, copy_x, copy_y = tree(t, slot)

            @pl.when(valid & to_x)
            def _():
                copy_x.wait_send()

            @pl.when(valid & to_y)
            def _():
                copy_y.wait_send()

    for o in range(1, 16):
        cc = (c + o) % 16
        p5_copy(o, cc, cc).wait_recv()
    for o in range(1, 16):
        p5_copy(o, (c + o) % 16, c).wait_send()

    @pl.when(own & (c < 8))
    def _():
        for o in range(1, 4):
            q = (z_hi + o) % 4
            g3_copy(o, z, q).wait_recv()

    @pl.when(other & (c < 8))
    def _():
        for q in range(4):
            g3_copy(1, z, q).wait_recv()

    push_g4()

    @pl.when(own)
    def _():
        for o in range(1, 8):
            p4_copy(o, (z + o) % 8, z_hi).wait_send()

    def outer(p, carry):
        sweep_step(pv, p, lambda i: x_slot(5 * (p - 1) + i))
        x_slot(5 * (p - 1) + 4)
        for k in range(4):
            @pl.when(p == k)
            def _():
                stage(k)
        to_root(p)

        @pl.when(p == 2)
        def _():
            raw_copy(0).start()

        return carry

    lax.fori_loop(0, 4, outer, 0)
    raw_copy(1).start()
    raw_copy(2).start()

    for o in range(1, 16):
        cc = (c + o) % 16

        @pl.when(cc < 8)
        def _():
            g4_copy(o, cc, jnp.where(cc < 8, cc, 0)).wait_recv()

    for k in range(3):
        for q in range(4):
            for cc in range(8):
                g[k, 64 * q + 8 * cc : 64 * q + 8 * cc + 8, :] = gp[cc, k, 8 * q : 8 * q + 8, :]

    x_slot(15)
    gq = g[0:2].reshape(512, TILE)
    us = -dot6(pv[...], gq, ROW_BY_COL)
    u[s] = us
    mparts[s] = g[2] - dot6(gq, us, COL_BY_COL)

    def swap(k, ref, e):
        return copy(ref.at[e], ref.at[e], s_sw.at[k], r_sw.at[k], sibling)

    def swap_r(e):
        return copy(r_buf.at[pl.ds(2 * e, 2)], r_buf.at[pl.ds(2 * e, 2)], s_sw.at[2], r_sw.at[2], sibling)

    swap(1, mparts, s).start()
    swap(0, u, s).start()
    x_slot(16)

    t0, t1 = piv[s, 0], piv[s, 1]

    def r_step(k, carry):
        cols = pl.ds(pl.multiple_of(k * 256, 256), 256)
        first = c * 768 + k * 256
        ya = modified(y[0, :, cols], t0, t1, first)
        yb = modified(y[1, :, cols], t1, t0, first)
        rk = -dot6(pv[...], jnp.concatenate([ya, yb], axis=0), ROW_BY_COL)
        r_buf[2 * s, :, cols] = rk[:TILE]
        r_buf[2 * s + 1, :, cols] = rk[TILE:]
        pparts[s, :, cols] = y[2, :, cols] - dot6(g[0:2].reshape(512, TILE), rk, COL_BY_COL)
        x_slot(17 + k)
        return carry

    lax.fori_loop(0, 3, r_step, 0)
    swap_r(s).start()
    swap(3, pparts, s).start()

    swap(1, mparts, 1 - s).wait_recv()
    n_buf[...] = mparts[0] + mparts[1]

    def outer_lead(p, carry):
        def two_slots(i):
            k = 4 * p + i
            first, last = (7 * k) // 4, (7 * (k + 1)) // 4
            x_slot(20 + first)
            x_slot(jnp.where(last - first == 2, 21 + first, -1))

        sweep_step(n_buf, p, two_slots)
        return carry

    lax.fori_loop(0, 2, outer_lead, 0)
    swap(0, u, 1 - s).wait_recv()

    swap_r(1 - s).wait_recv()
    swap(3, pparts, 1 - s).wait_recv()
    p0c_buf[...] = pparts[0] + pparts[1]

    def last_step(k, carry):
        cols = pl.ds(pl.multiple_of(k * 256, 256), 256)
        rows = span(k * 256, 256)
        first = k_own * 768 + k * 256
        lead = x_buf[4, :, cols]
        total = jnp.zeros((TILE, 768), F32)
        for e in range(2):
            ta, tb = piv[e, 0], piv[e, 1]
            xa = modified(x_buf[2 * e, :, cols], ta, tb, first)
            xb = modified(x_buf[2 * e + 1, :, cols], tb, ta, first)
            x = jnp.concatenate([xa, xb], axis=0)
            lead = lead - dot6(u[e], x, COL_BY_COL)
            total = total - dot3(x, r_buf[2 * e : 2 * e + 2].reshape(512, 768), COL_BY_COL)
        low = -dot6(lead, n_buf[...], COL_BY_COL)
        low_out[rows, :] = low
        keep = (first + iota((TILE, 768), 0) < TILE) | (col_ids < TILE)
        corr[rows, :] = total - jnp.where(keep, 0.0, dot3(low, p0c_buf[...], ROW_BY_COL))
        return carry

    lax.fori_loop(0, 3, last_step, 0)

    @pl.when(other)
    def _():
        merge_p().wait_send()
        merge_c().wait_send()
        Ring(0, 1).both("wait_send")
        Ring(1, -1).both("wait_send")
        Ring(2, 1).both("wait_send")

    @pl.when(sends_h)
    def _():
        h_first().wait_send()

    @pl.when(own)
    def _():
        for o in range(1, 16):
            p2_copy(o, (c + o) % 16, c).wait_send()
        for o in range(1, 4):
            rs_copy(o, (z_hi + o) % 4, z_hi).wait_send()
            p3_copy(o, (z_hi + o) % 4, z_hi).wait_send()

        @pl.when(leads_h)
        def _():
            for q in range(1, 4):
                h_copy(q).wait_send()

        @pl.when(c == 0)
        def _():
            for o in range(1, 4):
                g1_copy(o, (z_hi + o) % 4, z_hi).wait_send()
            for cc in range(1, 8):
                g2_copy(cc).wait_send()

        @pl.when(c < 8)
        def _():
            for o in range(1, 8):
                g3_copy(o, (z + o) % 8, z_hi).wait_send()

        Ring(0, 1).both("wait_send")
        Ring(0, -1).both("wait_send")
        Ring(1, 1).both("wait_send")
        Ring(2, -1).both("wait_send")

    @pl.when(c < 8)
    def _():
        for o in range(1, 16):
            g4_copy(o, (c + o) % 16, c).wait_send()

    @pl.when(c == k_sib)
    def _():
        for k in range(4):
            sib_panels(s, k).wait_send()

            @pl.when(s == 0)
            def _():
                sib_h(k).wait_send()

    def x_last(slot, carry):
        x_end(slot)
        return carry

    lax.fori_loop(0, 34, x_last, 0)
    swap(0, u, s).wait_send()
    swap(1, mparts, s).wait_send()
    swap_r(s).wait_send()
    swap(3, pparts, s).wait_send()
    for k in range(3):
        raw_copy(k).wait()


def run_main(prior, shift, pivots):
    vmem = pl.BlockSpec(memory_space=pltpu.VMEM)
    dma = pltpu.SemaphoreType.DMA
    return pl.pallas_call(
        main_kernel,
        out_shape=(
            jax.ShapeDtypeStruct((768, 768), F32),
            jax.ShapeDtypeStruct((768, 768), F32),
            jax.ShapeDtypeStruct((768, 256), F32),
        ),
        in_specs=[vmem, vmem, pl.BlockSpec(memory_space=pl.ANY), pl.BlockSpec(memory_space=pltpu.SMEM)],
        out_specs=(pl.BlockSpec(memory_space=pl.ANY), vmem, vmem),
        scratch_shapes=[
            pltpu.VMEM((5, 256, 768), F32),
            pltpu.VMEM((4, 256, 768), F32),
            pltpu.VMEM((256, 768), F32),
            pltpu.VMEM((256, 256), F32),
            pltpu.VMEM((3, 256, 768), F32),
            pltpu.VMEM((512, 512), F32),
            pltpu.VMEM((3, 256, 768), F32),
            pltpu.VMEM((512, 512), F32),
            pltpu.VMEM((4, 2, 64, 768), F32),
            pltpu.VMEM((3, 256, 768), F32),
            pltpu.VMEM((256, 768), F32),
            pltpu.VMEM((16, 32, 512), F32),
            pltpu.VMEM((32, 512), F32),
            pltpu.VMEM((4, 8, 512), F32),
            pltpu.VMEM((512, 512), F32),
            pltpu.VMEM((4, 3, 64, 256), F32),
            pltpu.VMEM((3, 64, 256), F32),
            pltpu.VMEM((8, 3, 32, 256), F32),
            pltpu.VMEM((3, 256, 256), F32),
            pltpu.VMEM((2, 512, 256), F32),
            pltpu.VMEM((2, 256, 256), F32),
            pltpu.VMEM((2, 256, 768), F32),
            dma((2,)), dma((2,)), dma((2,)),
            dma((15,)), dma((16,)), dma((3,)), dma((4,)), dma((7,)), dma((4,)), dma((15,)), dma((16,)),
            dma((3,)), dma((4,)), dma((7,)), dma((1,)), dma((7,)), dma((4,)), dma((15,)), dma((8,)),
            dma((3,)), dma((4,)), dma((3,)), dma((1,)),
            dma((4,)), dma((4,)), dma((4,)), dma((4,)), dma((4,)), dma((4,)),
            dma((4,)), dma((4,)), dma((4,)), dma((4,)),
            dma((4, 20)), dma((4, 20)), dma((4, 20)),
            dma((3,)), dma((3,)), dma((4,)), dma((4,)),
        ],
        compiler_params=pltpu.CompilerParams(
            collective_id=0, has_side_effects=True, vmem_limit_bytes=56 * 1024 * 1024
        ),
    )(prior, shift, prior, pivots)


def final_kernel(place, piv, own, raw, corr, low, shift, schur, lower):
    step = pl.program_id(0)
    rows = place[1] * 768 + step * 256 + iota((256, 768), 0)
    cols = place[2] * 768 + iota((256, 768), 1)
    added = jnp.where(rows == cols, shift[...], 0.0)
    row_tile, col_tile = rows // TILE, cols // TILE

    def zeroed(block, e):
        a, b = piv[e, 0], piv[e, 1]
        hit = (row_tile == a) | (row_tile == b) | (col_tile == a) | (col_tile == b)
        return jnp.where(hit, 0.0, block + added)

    schur[0, 0] = zeroed(own[0], place[0]) + zeroed(raw[...], 1 - place[0]) + corr[...]
    lower[0, 0] = low[...]


def run_final(place, pivots, prior, raw, corr, low, shift):
    spec = pltpu.PrefetchScalarGridSpec(
        num_scalar_prefetch=2,
        grid=(3,),
        in_specs=[
            pl.BlockSpec((1, 256, 768), lambda i, p, v: (0, 3 * p[0] + i, 0)),
            pl.BlockSpec((256, 768), lambda i, p, v: (i, 0)),
            pl.BlockSpec((256, 768), lambda i, p, v: (i, 0)),
            pl.BlockSpec((256, 256), lambda i, p, v: (i, 0)),
            pl.BlockSpec((1, 768), lambda i, p, v: (0, 0)),
        ],
        out_specs=(
            pl.BlockSpec((1, 1, 256, 768), lambda i, p, v: (0, 0, i, 0)),
            pl.BlockSpec((1, 1, 256, 256), lambda i, p, v: (0, 0, i, 0)),
        ),
    )
    return pl.pallas_call(
        final_kernel,
        grid_spec=spec,
        out_shape=(
            jax.ShapeDtypeStruct((1, 1, 768, 768), F32),
            jax.ShapeDtypeStruct((1, 1, 768, 256), F32),
        ),
        compiler_params=pltpu.CompilerParams(vmem_limit_bytes=56 * 1024 * 1024),
    )(place, pivots, prior, raw, corr, low, shift)


def shifts(quantum):
    quantum = quantum.astype(F32)
    return (
        0.025 * quantum[:, 0] * (quantum[:, 0] + 1.0)
        + 0.01 * quantum[:, 1] * quantum[:, 1]
        + 0.01 * quantum[:, 2] * (quantum[:, 2] + 1.0)
        + 0.005 * quantum[:, 3] * (quantum[:, 3] + 1.0)
    )


def per_device(prior_y, labels, pivots):
    r, c, d = lax.axis_index("row"), lax.axis_index("col"), lax.axis_index("dir")
    shift = shifts(lax.dynamic_slice_in_dim(labels, c * 768, 768, 0))[None, :]
    raw, corr, low = run_main(prior_y, shift, pivots)
    place = jnp.stack([d, 2 * r + d, c]).astype(jnp.int32)
    return run_final(place, pivots, prior_y, raw, corr, low, shift)


def solution(mesh):
    placed = (P("dir", "row", "col"), P(), P())
    return jax.shard_map(
        per_device,
        mesh=mesh,
        in_specs=placed,
        out_specs=(P("row", "dir", None, "col"), P("row", "dir", None, None)),
        check_vma=False,
    )
```

```python
import functools

import jax
import jax.numpy as jnp
from jax import lax
from jax.experimental import pallas as pl
from jax.experimental.pallas import tpu as pltpu
from jax.sharding import PartitionSpec as P

TILE = 256
F32 = jnp.float32
BF16 = jnp.bfloat16
MESH = pl.DeviceIdType.MESH
ROW_BY_COL = ((1,), (0,))
COL_BY_COL = ((0,), (0,))


def dot6(a, b, dims):
    return lax.dot_general(
        a, b, (dims, ((), ())), precision=lax.Precision.HIGHEST, preferred_element_type=F32
    )


def split(x):
    high = x.astype(BF16)
    return high, (x - high.astype(F32)).astype(BF16)


def dot3(a, b, dims):
    ah, al = split(a)
    bh, bl = split(b)

    def one(p, q):
        return lax.dot_general(p, q, (dims, ((), ())), preferred_element_type=F32)

    return one(ah, bh) + (one(ah, bl) + one(al, bh))


def iota(shape, dim):
    return lax.broadcasted_iota(jnp.int32, shape, dim)


def sweep128(block, service, group=4):
    lanes, subs = iota((8, 128), 1), iota((8, 128), 0)
    width = 8 * group
    hits = [subs == k for k in range(8)]

    def body(step, b):
        service(step)
        s = [b[8 * j : 8 * j + 8, :] for j in range(group)]
        for i in range(group):
            v = [jnp.broadcast_to(s[i][:, 8 * i + m : 8 * i + m + 1], (8, 128)) for m in range(8)]
            for k in range(8):
                vk = v[k]
                inv = 1.0 / vk[k : k + 1, :]
                for j in range(8):
                    if j != k:
                        rj = v[j][k : k + 1, :] * inv
                        v[j] = jnp.where(hits[k], rj, v[j] - vk * rj)
                v[k] = jnp.where(hits[k], -inv, vk * inv)
            inside = (lanes >= 8 * i) & (lanes < 8 * i + 8)
            x = jnp.where(inside, jnp.where(lanes - 8 * i == subs, -1.0, 0.0), s[i])
            r = -v[0] * x[0:1, :]
            for m in range(1, 8):
                r = r - v[m] * x[m : m + 1, :]
            for q in range(1, group):
                j = (i + q) % group
                acc = jnp.where(inside, 0.0, s[j])
                for m in range(8):
                    col = jnp.broadcast_to(s[j][:, 8 * i + m : 8 * i + m + 1], (8, 128))
                    acc = acc - col * r[m : m + 1, :]
                s[j] = acc
            s[i] = r
        r = jnp.concatenate(s, axis=0)
        rest = b[width:, :]
        lane = iota(rest.shape, 1)
        rest = jnp.where(lane < width, 0.0, rest) - dot6(rest[:, :width], r, ROW_BY_COL)
        return pltpu.roll(jnp.concatenate([rest, r], axis=0), 128 - width, 1)

    return lax.fori_loop(0, 128 // width, body, block)


def sweep_step(a_ref, p, service):
    n = a_ref.shape[0]
    at = pl.multiple_of(p * 128, 128)
    neg = sweep128(a_ref[pl.ds(at, 128), pl.ds(at, 128)], service)
    x = a_ref[pl.ds(at, 128), :]
    col, row = iota((128, n), 1), iota((128, n), 0)
    x = jnp.where(col // 128 == p, jnp.where(col - at == row, -1.0, 0.0), x)
    r = -dot6(neg, x, ROW_BY_COL)
    a_ref[pl.ds(at, 128), :] = jnp.zeros((128, n), F32)
    a_ref[:, pl.ds(at, 128)] = jnp.zeros((n, 128), F32)
    a_ref[...] = a_ref[...] - dot6(x, r, COL_BY_COL)


def modified(panel, tile, other, col_first):
    ids = col_first + iota(panel.shape, 1)
    local = ids - tile * TILE
    own = (local >= 0) & (local < TILE)
    beside = ids - other * TILE
    gone = (beside >= 0) & (beside < TILE)
    panel = jnp.where(own, jnp.where(local == iota(panel.shape, 0), -1.0, 0.0), panel)
    return jnp.where(gone, 0.0, panel)


def main_kernel(
    a_ref, shift, piv,
    schur, lower,
    raw,     x_buf, r_buf, p0c_buf, n_buf, cand, pcand, cm, pm, rs1, rs2, acc, y, hpre, p2, p2sum, p3, pv, gr, gsum, gp, g, u, mparts, pparts,
    sem_p1, sem_c1, sem_h1, s_p2, r_p2, s_p3, r_p3, s_p4, r_p4, s_p5, r_p5,
    s_g1, r_g1, s_g2, r_g2, s_g3, r_g3, s_g4, r_g4,
    s_rs, r_rs, s_h, r_h, s_agr, s_agl, r_ag, s_ahr, s_ahl, r_ah,
    s_sib, r_sib, s_sibh, r_sibh, s_xa, s_xb, r_x, s_raw, r_raw, s_sw, r_sw,
):
    d, r, c = lax.axis_index("dir"), lax.axis_index("row"), lax.axis_index("col")
    s, z_hi = r % 2, r // 2
    z = 2 * z_hi + d
    cx, cy = c % 4, c // 4
    own = s == d
    other = s != d

    def at(zz, cc):
        return (zz % 2, 2 * (zz // 2) + s, cc)

    sibling = (d, r + 1 - 2 * s, c)
    partner = (1 - d, r, c)

    def copy(src, dst, send, recv, device):
        return pltpu.make_async_remote_copy(
            src_ref=src, dst_ref=dst, send_sem=send, recv_sem=recv, device_id=device, device_id_type=MESH
        )

    def span(first, count):
        return pl.ds(pl.multiple_of(first, 8), count)

    barrier = pltpu.get_barrier_semaphore()
    pl.semaphore_signal(barrier, inc=1, device_id=sibling, device_id_type=MESH)
    for o in range(1, 8):
        pl.semaphore_signal(barrier, inc=1, device_id=at((z + o) % 8, c), device_id_type=MESH)
    for o in range(1, 16):
        pl.semaphore_signal(barrier, inc=1, device_id=at(z, (c + o) % 16), device_id_type=MESH)

    tiles = (piv[d, 0], piv[d, 1])
    col_ids = c * 768 + iota((TILE, 768), 1)
    for k in range(2):
        named = jnp.full((TILE, 768), tiles[k], jnp.int32)
        block = jnp.zeros((TILE, 768), F32)
        for j in range(6):
            block = jnp.where(named == 6 * r + j, a_ref[0, TILE * j : TILE * j + TILE, :], block)
        ids = tiles[k] * TILE + iota((TILE, 768), 0)
        here = (ids == col_ids) & (ids >= r * 1536) & (ids < r * 1536 + 1536)
        cand[k] = block + jnp.where(here, shift[...], 0.0)
    lead = a_ref[0, 0:TILE, :] + jnp.where(iota((TILE, 768), 0) == col_ids, shift[...], 0.0)
    gone = (col_ids // TILE == tiles[0]) | (col_ids // TILE == tiles[1]) | (iota((TILE, 768), 0) + r * 1536 >= 1536)
    cand[2] = jnp.where(gone, 0.0, lead)
    for k in range(2):
        named = jnp.full((2 * TILE, TILE), tiles[k], jnp.int32)
        block = jnp.zeros((2 * TILE, TILE), F32)
        for j in range(3):
            part = cand[0:2, :, TILE * j : TILE * j + TILE].reshape(2 * TILE, TILE)
            block = jnp.where(named == 3 * c + j, part, block)
        pcand[:, TILE * k : TILE * k + TILE] = block
    pl.semaphore_wait(barrier, 23)

    def merge_p():
        return copy(pcand, pm, sem_p1.at[0], sem_p1.at[1], sibling)

    def merge_c():
        return copy(cand.at[pl.ds(0, 2)], cm.at[pl.ds(0, 2)], sem_c1.at[0], sem_c1.at[1], sibling)

    def h_first():
        return copy(cand.at[2], hpre, sem_h1.at[0], sem_h1.at[1], partner)

    def p2_copy(o, cc, slot):
        return copy(pm.at[span(32 * cc, 32), :], p2.at[slot], s_p2.at[o - 1], r_p2.at[slot], at(z, cc))

    def rs_first(way, layer):
        q = (layer + 2) % 4
        k = (1 - way) // 2
        return copy(
            cm.at[pl.ds(0, 2), span(64 * q + 32 * k, 32), :], rs1.at[k], s_rs.at[k], r_rs.at[k],
            at(2 * ((layer + way + 4) % 4) + d, c),
        )

    def rs_second(way, layer):
        q = (layer + way + 4) % 4
        k = (1 - way) // 2
        return copy(
            acc.at[k], rs2.at[k], s_rs.at[2 + k], r_rs.at[2 + k], at(2 * q + d, c)
        )

    def h_copy(q):
        rows = span(64 * q, 64)
        return copy(cm.at[2, rows, :], y.at[2, rows, :], s_h.at[q - 1], r_h.at[0], at(2 * q + d, c))

    def p3_copy(o, q, slot):
        return copy(p2sum.at[span(8 * q, 8), :], p3.at[slot], s_p3.at[o - 1], r_p3.at[slot], at(2 * q + d, c))

    def p4_copy(o, zz, slot):
        rows = span(32 * c + 8 * slot, 8)
        return copy(pv.at[rows, :], pv.at[rows, :], s_p4.at[o - 1], r_p4.at[slot], at(zz, c))

    def p5_copy(o, cc, slot):
        rows = span(32 * slot, 32)
        return copy(pv.at[rows, :], pv.at[rows, :], s_p5.at[o - 1], r_p5.at[slot], at(z, cc))

    def g1_copy(o, q, slot):
        return copy(
            cm.at[:, span(64 * q, 64), pl.ds(0, TILE)], gr.at[slot], s_g1.at[o - 1], r_g1.at[slot], at(2 * q + d, c)
        )

    def g2_copy(cc):
        return copy(
            gsum.at[:, span(8 * cc, 8), :], gp.at[cc, :, span(8 * z_hi, 8), :], s_g2.at[cc - 1], r_g2.at[0], at(z, cc)
        )

    def g3_copy(o, zz, slot):
        block = gp.at[c, :, span(8 * slot, 8), :]
        return copy(block, block, s_g3.at[o - 1], r_g3.at[slot], at(zz, c))

    def g4_copy(o, cc, slot):
        return copy(gp.at[slot], gp.at[slot], s_g4.at[o - 1], r_g4.at[slot], at(z, cc))

    def raw_copy(k):
        return copy(
            a_ref.at[0, span((1 - d) * 768 + 128 * k, 128), :],
            raw.at[pl.ds(128 * k, 128), :], s_raw.at[k], r_raw.at[k], partner,
        )

    sends_h = (d == 1) & (r == 0)
    leads_h = (d == 0) & (r == 0)

    @pl.when(other)
    def _():
        merge_p().start()
        merge_c().start()

    @pl.when(sends_h)
    def _():
        h_first().start()

    raw_copy(0).start()

    @pl.when(s == 1)
    def _():
        y[2] = jnp.zeros((TILE, 768), F32)

    def push_g4():
        @pl.when(c < 8)
        def _():
            for o in range(1, 16):
                g4_copy(o, (c + o) % 16, c).start()

    @pl.when(own)
    def _():
        merge_p().wait_recv()
        pm[...] = pm[...] + pcand[...]
        for o in range(1, 16):
            p2_copy(o, (c + o) % 16, c).start()
        merge_c().wait_recv()
        cm[0:2] = cm[0:2] + cand[0:2]

        @pl.when(leads_h)
        def _():
            h_first().wait_recv()
            cm[2] = cand[2] + hpre[...]

        @pl.when(r != d)
        def _():
            cm[2] = jnp.zeros((TILE, 768), F32)

        @pl.when((r == d) & (d == 1))
        def _():
            cm[2] = jnp.zeros((TILE, 768), F32)

        total = pm[span(32 * c, 32), :]
        for o in range(1, 16):
            cc = (c + o) % 16
            p2_copy(o, cc, cc).wait_recv()
            total = total + p2[cc]
        p2sum[...] = total
        for o in range(1, 4):
            p3_copy(o, (z_hi + o) % 4, z_hi).start()

        total = p2sum[span(8 * z_hi, 8), :]
        for o in range(1, 4):
            q = (z_hi + o) % 4
            p3_copy(o, q, q).wait_recv()
            total = total + p3[q]
        pv[span(32 * c + 8 * z_hi, 8), :] = total
        for o in range(1, 8):
            p4_copy(o, (z + o) % 8, z_hi).start()

        @pl.when(c == 0)
        def _():
            for o in range(1, 4):
                g1_copy(o, (z_hi + o) % 4, z_hi).start()

        for way in (1, -1):
            rs_first(way, z_hi).start()

        @pl.when(leads_h)
        def _():
            for q in range(1, 4):
                h_copy(q).start()
            y[2, 0:64, :] = cm[2, 0:64, :]

        for o in range(1, 4):
            q = (z_hi + o) % 4
            p4_copy(o, z, q).wait_recv()

    @pl.when(other)
    def _():
        for q in range(4):
            p4_copy(1, z, q).wait_recv()

    for o in range(1, 16):
        p5_copy(o, (c + o) % 16, c).start()

    @pl.when(own)
    def _():
        for way in (1, -1):
            k = (1 - way) // 2
            rs_first(way, z_hi).wait_recv()
            acc[k] = cm[0:2, span(64 * ((z_hi + way + 4) % 4), 64), :]
            acc[k, :, 32 * k : 32 * k + 32, :] = acc[k, :, 32 * k : 32 * k + 32, :] + rs1[k]
            rs_second(way, z_hi).start()

    def order(e, k):
        delta = jnp.where(
            e == d,
            jnp.where(k == 0, 0, jnp.where(k == 1, 2, jnp.where(k == 2, 6, 4))),
            jnp.where(k == 0, 1, jnp.where(k == 1, 7, jnp.where(k == 2, 3, 5))),
        )
        return (((z - (1 - 2 * e) * delta + 16) % 8 - e + 8) // 2) % 4

    class Ring:
        def __init__(self, k, step):
            q = order(s, k)
            rows = span(64 * q, 64)
            right = step == 1
            to = at((z + step * (1 - 2 * s) + 8) % 8, c)
            block = y.at[pl.ds(0, 2), rows, :]
            self.main = copy(block, block, (s_agr if right else s_agl).at[q], r_ag.at[q], to)
            block = y.at[2, rows, :]
            self.lead = copy(block, block, (s_ahr if right else s_ahl).at[q], r_ah.at[q], to)

        def both(self, name):
            getattr(self.main, name)()

            @pl.when(s == 0)
            def _():
                getattr(self.lead, name)()

    def arrive(k):
        Ring(k, 1).both("wait_recv")

    def stage(k):
        if k == 0 or k == 2:
            @pl.when(other)
            def _():
                arrive(k)
                Ring(k, 1).both("start")
                arrive(k + 1)
                if k == 0:
                    Ring(k + 1, -1).both("start")
        elif k == 1:
            @pl.when(own)
            def _():
                arrive(1)
                Ring(1, 1).both("start")
                arrive(2)
                Ring(2, -1).both("start")
        else:
            @pl.when(own)
            def _():
                arrive(3)

    k_own = 2 * r + d
    k_sib = 2 * (r + 1 - 2 * s) + d
    xs, ys = k_own % 4, k_own // 4

    def sib_panels(e, k):
        rows = span(64 * order(e, k), 64)
        return copy(
            y.at[pl.ds(0, 2), rows, :], x_buf.at[pl.ds(2 * e, 2), rows, :], s_sib.at[k], r_sib.at[k], sibling
        )

    def sib_h(k):
        rows = span(64 * order(0, k), 64)
        return copy(y.at[2, rows, :], x_buf.at[4, rows, :], s_sibh.at[k], r_sibh.at[k], sibling)

    def to_root(k):
        @pl.when(c == k_sib)
        def _():
            sib_panels(s, k).start()

            @pl.when(s == 0)
            def _():
                sib_h(k).start()

        @pl.when(c == k_own)
        def _():
            rows = span(64 * order(s, k), 64)
            x_buf[pl.ds(2 * s, 2), rows, :] = y[0:2, rows, :]

            @pl.when(s == 0)
            def _():
                x_buf[4, rows, :] = y[2, rows, :]

            sib_panels(1 - s, k).wait_recv()

            @pl.when(s == 1)
            def _():
                sib_h(k).wait_recv()

    def tree(t, slot):
        way = 1 if t % 2 == 0 else -1
        dx = (way * (cx - xs) + 4) % 4
        dy = (way * (cy - ys) + 4) % 4
        depth = dx + dy
        if t < 2:
            to_x = (dy == 0) & (dx < 3)
            to_y = dy < 3
        else:
            to_x = (dy >= 1) & (dx < 3)
            to_y = ((dx == 0) & (dy < 3)) | ((dx >= 1) & (dy == 3))
            depth = depth + jnp.where((dy == 0) & (dx >= 1), 4, 0)
        p = slot - 2 * depth
        valid = (p >= 0) & (p < 20)
        p = jnp.where(valid, p, 0)
        tile = p % 5
        rows = span(64 * order(jnp.where(tile == 4, 0, tile // 2), p // 5) + 16 * t, 16)
        block = x_buf.at[tile, rows, :]
        next_x = at(z, 4 * cy + (cx + way + 4) % 4)
        next_y = at(z, 4 * ((cy + way + 4) % 4) + cx)
        copy_x = copy(block, block, s_xa.at[t, p], r_x.at[t, p], next_x)
        copy_y = copy(block, block, s_xb.at[t, p], r_x.at[t, p], next_y)
        return valid, depth, to_x, to_y, copy_x, copy_y

    def x_slot(slot):
        for t in range(4):
            valid, depth, to_x, to_y, copy_x, copy_y = tree(t, slot)

            @pl.when(valid & (depth > 0))
            def _():
                copy_x.wait_recv()

            @pl.when(valid & to_x)
            def _():
                copy_x.start()

            @pl.when(valid & to_y)
            def _():
                copy_y.start()

    def x_end(slot):
        for t in range(4):
            valid, _, to_x, to_y, copy_x, copy_y = tree(t, slot)

            @pl.when(valid & to_x)
            def _():
                copy_x.wait_send()

            @pl.when(valid & to_y)
            def _():
                copy_y.wait_send()

    for o in range(1, 16):
        cc = (c + o) % 16
        p5_copy(o, cc, cc).wait_recv()
    for o in range(1, 16):
        p5_copy(o, (c + o) % 16, c).wait_send()

    @pl.when(own)
    def _():
        for o in range(1, 8):
            p4_copy(o, (z + o) % 8, z_hi).wait_send()

    def end_reduce():
        @pl.when(own)
        def _():
            rows = span(64 * z_hi, 64)
            total = cm[0:2, rows, :]
            for way in (1, -1):
                rs_second(way, z_hi).wait_recv()
                total = total + rs2[(1 - way) // 2]
            y[0:2, rows, :] = total

            @pl.when((d == 0) & (r != 0))
            def _():
                h_copy(z_hi).wait_recv()

            Ring(0, 1).both("start")
            Ring(0, -1).both("start")

    @pl.when(own)
    def _():
        @pl.when(c == 0)
        def _():
            total = cm[:, span(64 * z_hi, 64), 0:TILE]
            for o in range(1, 4):
                q = (z_hi + o) % 4
                g1_copy(o, q, q).wait_recv()
                total = total + gr[q]
            gsum[...] = total
            for cc in range(1, 8):
                g2_copy(cc).start()
            gp[0, :, span(8 * z_hi, 8), :] = total[:, 0:8]

    def between(p, i):
        @pl.when((p == 0) & (i == 2) & own)
        def _():
            @pl.when((c > 0) & (c < 8))
            def _():
                g2_copy(c).wait_recv()

            @pl.when(c < 8)
            def _():
                for o in range(1, 8):
                    g3_copy(o, (z + o) % 8, z_hi).start()

        x_slot(5 * (p - 2) + i)

    def outer(p, carry):
        sweep_step(pv, p, lambda i: between(p, i))
        x_slot(5 * (p - 2) + 4)

        @pl.when(p == 0)
        def _():
            end_reduce()

        for k in range(3):
            @pl.when(p == k + 1)
            def _():
                stage(k)

        @pl.when(p >= 1)
        def _():
            to_root(p - 1)

        @pl.when(p == 1)
        def _():
            @pl.when(own & (c < 8))
            def _():
                for o in range(1, 4):
                    q = (z_hi + o) % 4
                    g3_copy(o, z, q).wait_recv()

            @pl.when(other & (c < 8))
            def _():
                for q in range(4):
                    g3_copy(1, z, q).wait_recv()

            push_g4()

        return carry

    lax.fori_loop(0, 4, outer, 0)
    x_slot(10)

    for o in range(1, 16):
        cc = (c + o) % 16

        @pl.when(cc < 8)
        def _():
            g4_copy(o, cc, jnp.where(cc < 8, cc, 0)).wait_recv()

    for k in range(3):
        for q in range(4):
            for cc in range(8):
                g[k, 64 * q + 8 * cc : 64 * q + 8 * cc + 8, :] = gp[cc, k, 8 * q : 8 * q + 8, :]

    x_slot(11)
    gq = g[0:2].reshape(512, TILE)
    us = -dot6(pv[...], gq, ROW_BY_COL)
    u[s] = us
    mparts[s] = g[2] - dot6(gq, us, COL_BY_COL)

    def swap(k, ref, e):
        return copy(ref.at[e], ref.at[e], s_sw.at[k], r_sw.at[k], sibling)

    def swap_r(e):
        return copy(r_buf.at[pl.ds(2 * e, 2)], r_buf.at[pl.ds(2 * e, 2)], s_sw.at[2], r_sw.at[2], sibling)

    swap(1, mparts, s).start()
    swap(0, u, s).start()
    stage(3)
    for k in range(1, 6):
        raw_copy(k).start()
    to_root(3)
    x_slot(12)
    x_slot(13)

    t0, t1 = piv[s, 0], piv[s, 1]

    def r_step(k, carry):
        cols = pl.ds(pl.multiple_of(k * 256, 256), 256)
        first = c * 768 + k * 256
        ya = modified(y[0, :, cols], t0, t1, first)
        yb = modified(y[1, :, cols], t1, t0, first)
        rk = -dot6(pv[...], jnp.concatenate([ya, yb], axis=0), ROW_BY_COL)
        r_buf[2 * s, :, cols] = rk[:TILE]
        r_buf[2 * s + 1, :, cols] = rk[TILE:]
        pparts[s, :, cols] = y[2, :, cols] - dot6(g[0:2].reshape(512, TILE), rk, COL_BY_COL)
        x_slot(14 + k)
        return carry

    lax.fori_loop(0, 3, r_step, 0)
    swap_r(s).start()
    swap(3, pparts, s).start()

    swap(1, mparts, 1 - s).wait_recv()
    n_buf[...] = mparts[0] + mparts[1]

    def outer_lead(p, carry):
        def two_slots(i):
            x_slot(17 + 8 * p + 2 * i)
            x_slot(18 + 8 * p + 2 * i)

        sweep_step(n_buf, p, two_slots)
        return carry

    lax.fori_loop(0, 2, outer_lead, 0)
    x_slot(33)
    swap(0, u, 1 - s).wait_recv()

    swap_r(1 - s).wait_recv()
    swap(3, pparts, 1 - s).wait_recv()
    p0c_buf[...] = pparts[0] + pparts[1]

    for k in range(6):
        raw_copy(k).wait()

    def zeroed(block, ids, e):
        ta, tb = piv[e, 0], piv[e, 1]
        block = block + jnp.where(ids == col_ids, shift[...], 0.0)
        row_tile, col_tile = ids // TILE, col_ids // TILE
        hit = (row_tile == ta) | (row_tile == tb) | (col_tile == ta) | (col_tile == tb)
        return jnp.where(hit, 0.0, block)

    def last_step(k, carry):
        cols = pl.ds(pl.multiple_of(k * 256, 256), 256)
        rows = span(k * 256, 256)
        first = k_own * 768 + k * 256
        lead = x_buf[4, :, cols]
        ids = first + iota((TILE, 768), 0)
        mine = a_ref[0, span(d * 768 + k * 256, 256), :]
        total = zeroed(mine, ids, d) + zeroed(raw[rows, :], ids, 1 - d)
        for e in range(2):
            ta, tb = piv[e, 0], piv[e, 1]
            xa = modified(x_buf[2 * e, :, cols], ta, tb, first)
            xb = modified(x_buf[2 * e + 1, :, cols], tb, ta, first)
            x = jnp.concatenate([xa, xb], axis=0)
            lead = lead - dot6(u[e], x, COL_BY_COL)
            total = total - dot3(x, r_buf[2 * e : 2 * e + 2].reshape(512, 768), COL_BY_COL)
        low = -dot6(lead, n_buf[...], COL_BY_COL)
        lower[0, 0, rows, :] = low
        keep = (ids < TILE) | (col_ids < TILE)
        schur[0, 0, rows, :] = total - jnp.where(keep, 0.0, dot3(low, p0c_buf[...], ROW_BY_COL))
        return carry

    lax.fori_loop(0, 3, last_step, 0)

    @pl.when(other)
    def _():
        merge_p().wait_send()
        merge_c().wait_send()
        Ring(0, 1).both("wait_send")
        Ring(1, -1).both("wait_send")
        Ring(2, 1).both("wait_send")

    @pl.when(sends_h)
    def _():
        h_first().wait_send()

    @pl.when(own)
    def _():
        for o in range(1, 16):
            p2_copy(o, (c + o) % 16, c).wait_send()
        for way in (1, -1):
            rs_first(way, z_hi).wait_send()
            rs_second(way, z_hi).wait_send()
        for o in range(1, 4):
            p3_copy(o, (z_hi + o) % 4, z_hi).wait_send()

        @pl.when(leads_h)
        def _():
            for q in range(1, 4):
                h_copy(q).wait_send()

        @pl.when(c == 0)
        def _():
            for o in range(1, 4):
                g1_copy(o, (z_hi + o) % 4, z_hi).wait_send()
            for cc in range(1, 8):
                g2_copy(cc).wait_send()

        @pl.when(c < 8)
        def _():
            for o in range(1, 8):
                g3_copy(o, (z + o) % 8, z_hi).wait_send()

        Ring(0, 1).both("wait_send")
        Ring(0, -1).both("wait_send")
        Ring(1, 1).both("wait_send")
        Ring(2, -1).both("wait_send")

    @pl.when(c < 8)
    def _():
        for o in range(1, 16):
            g4_copy(o, (c + o) % 16, c).wait_send()

    @pl.when(c == k_sib)
    def _():
        for k in range(4):
            sib_panels(s, k).wait_send()

            @pl.when(s == 0)
            def _():
                sib_h(k).wait_send()

    def x_last(slot, carry):
        x_end(slot)
        return carry

    lax.fori_loop(0, 34, x_last, 0)
    swap(0, u, s).wait_send()
    swap(1, mparts, s).wait_send()
    swap_r(s).wait_send()
    swap(3, pparts, s).wait_send()


def run_main(prior, shift, pivots):
    vmem = pl.BlockSpec(memory_space=pltpu.VMEM)
    dma = pltpu.SemaphoreType.DMA
    return pl.pallas_call(
        main_kernel,
        out_shape=(
            jax.ShapeDtypeStruct((1, 1, 768, 768), F32),
            jax.ShapeDtypeStruct((1, 1, 768, TILE), F32),
        ),
        in_specs=[vmem, vmem, pl.BlockSpec(memory_space=pltpu.SMEM)],
        out_specs=(vmem, vmem),
        scratch_shapes=[
            pltpu.VMEM((768, 768), F32),
            pltpu.VMEM((5, 256, 768), F32),
            pltpu.VMEM((4, 256, 768), F32),
            pltpu.VMEM((256, 768), F32),
            pltpu.VMEM((256, 256), F32),
            pltpu.VMEM((3, 256, 768), F32),
            pltpu.VMEM((512, 512), F32),
            pltpu.VMEM((3, 256, 768), F32),
            pltpu.VMEM((512, 512), F32),
            pltpu.VMEM((2, 2, 32, 768), F32),
            pltpu.VMEM((2, 2, 64, 768), F32),
            pltpu.VMEM((2, 2, 64, 768), F32),
            pltpu.VMEM((3, 256, 768), F32),
            pltpu.VMEM((256, 768), F32),
            pltpu.VMEM((16, 32, 512), F32),
            pltpu.VMEM((32, 512), F32),
            pltpu.VMEM((4, 8, 512), F32),
            pltpu.VMEM((512, 512), F32),
            pltpu.VMEM((4, 3, 64, 256), F32),
            pltpu.VMEM((3, 64, 256), F32),
            pltpu.VMEM((8, 3, 32, 256), F32),
            pltpu.VMEM((3, 256, 256), F32),
            pltpu.VMEM((2, 512, 256), F32),
            pltpu.VMEM((2, 256, 256), F32),
            pltpu.VMEM((2, 256, 768), F32),
            dma((2,)), dma((2,)), dma((2,)),
            dma((15,)), dma((16,)), dma((3,)), dma((4,)), dma((7,)), dma((4,)), dma((15,)), dma((16,)),
            dma((3,)), dma((4,)), dma((7,)), dma((1,)), dma((7,)), dma((4,)), dma((15,)), dma((8,)),
            dma((4,)), dma((4,)), dma((3,)), dma((1,)),
            dma((4,)), dma((4,)), dma((4,)), dma((4,)), dma((4,)), dma((4,)),
            dma((4,)), dma((4,)), dma((4,)), dma((4,)),
            dma((4, 20)), dma((4, 20)), dma((4, 20)),
            dma((6,)), dma((6,)), dma((4,)), dma((4,)),
        ],
        compiler_params=pltpu.CompilerParams(
            collective_id=0, has_side_effects=True, vmem_limit_bytes=56 * 1024 * 1024
        ),
    )(prior, shift, pivots)


def shifts(quantum):
    quantum = quantum.astype(F32)
    return (
        0.025 * quantum[:, 0] * (quantum[:, 0] + 1.0)
        + 0.01 * quantum[:, 1] * quantum[:, 1]
        + 0.01 * quantum[:, 2] * (quantum[:, 2] + 1.0)
        + 0.005 * quantum[:, 3] * (quantum[:, 3] + 1.0)
    )


def per_device(prior_y, labels, pivots):
    first = lax.axis_index("col") * 768
    shift = shifts(lax.dynamic_slice_in_dim(labels, first, 768, 0))[None, :]
    return run_main(prior_y, shift, pivots)


def solution(mesh):
    placed = (P("dir", "row", "col"), P(), P())
    return jax.shard_map(
        per_device,
        mesh=mesh,
        in_specs=placed,
        out_specs=(P("row", "dir", None, "col"), P("row", "dir", None, None)),
        check_vma=False,
    )
```

```python
import functools

import jax
import jax.numpy as jnp
from jax import lax
from jax.experimental import pallas as pl
from jax.experimental.pallas import tpu as pltpu
from jax.sharding import PartitionSpec as P

TILE = 256
F32 = jnp.float32
BF16 = jnp.bfloat16
MESH = pl.DeviceIdType.MESH
ROW_BY_COL = ((1,), (0,))
COL_BY_COL = ((0,), (0,))


def dot6(a, b, dims):
    return lax.dot_general(
        a, b, (dims, ((), ())), precision=lax.Precision.HIGHEST, preferred_element_type=F32
    )


def split(x):
    high = x.astype(BF16)
    return high, (x - high.astype(F32)).astype(BF16)


def dot3(a, b, dims):
    ah, al = split(a)
    bh, bl = split(b)

    def one(p, q):
        return lax.dot_general(p, q, (dims, ((), ())), preferred_element_type=F32)

    return one(ah, bh) + (one(ah, bl) + one(al, bh))


def iota(shape, dim):
    return lax.broadcasted_iota(jnp.int32, shape, dim)


def sweep128(block, service, group=4):
    lanes, subs = iota((8, 128), 1), iota((8, 128), 0)
    width = 8 * group
    hits = [subs == k for k in range(8)]

    def body(step, b):
        service(step)
        s = [b[8 * j : 8 * j + 8, :] for j in range(group)]
        for i in range(group):
            v = [jnp.broadcast_to(s[i][:, 8 * i + m : 8 * i + m + 1], (8, 128)) for m in range(8)]
            for k in range(8):
                vk = v[k]
                inv = 1.0 / vk[k : k + 1, :]
                for j in range(8):
                    if j != k:
                        rj = v[j][k : k + 1, :] * inv
                        v[j] = jnp.where(hits[k], rj, v[j] - vk * rj)
                v[k] = jnp.where(hits[k], -inv, vk * inv)
            inside = (lanes >= 8 * i) & (lanes < 8 * i + 8)
            x = jnp.where(inside, jnp.where(lanes - 8 * i == subs, -1.0, 0.0), s[i])
            r = -v[0] * x[0:1, :]
            for m in range(1, 8):
                r = r - v[m] * x[m : m + 1, :]
            for q in range(1, group):
                j = (i + q) % group
                acc = jnp.where(inside, 0.0, s[j])
                for m in range(8):
                    col = jnp.broadcast_to(s[j][:, 8 * i + m : 8 * i + m + 1], (8, 128))
                    acc = acc - col * r[m : m + 1, :]
                s[j] = acc
            s[i] = r
        r = jnp.concatenate(s, axis=0)
        rest = b[width:, :]
        lane = iota(rest.shape, 1)
        rest = jnp.where(lane < width, 0.0, rest) - dot6(rest[:, :width], r, ROW_BY_COL)
        return pltpu.roll(jnp.concatenate([rest, r], axis=0), 128 - width, 1)

    return lax.fori_loop(0, 128 // width, body, block)


def sweep_step(a_ref, p, service):
    n = a_ref.shape[0]
    at = pl.multiple_of(p * 128, 128)
    neg = sweep128(a_ref[pl.ds(at, 128), pl.ds(at, 128)], service)
    x = a_ref[pl.ds(at, 128), :]
    col, row = iota((128, n), 1), iota((128, n), 0)
    x = jnp.where(col // 128 == p, jnp.where(col - at == row, -1.0, 0.0), x)
    r = -dot6(neg, x, ROW_BY_COL)
    a_ref[pl.ds(at, 128), :] = jnp.zeros((128, n), F32)
    a_ref[:, pl.ds(at, 128)] = jnp.zeros((n, 128), F32)
    a_ref[...] = a_ref[...] - dot6(x, r, COL_BY_COL)


def modified(panel, tile, other, col_first):
    ids = col_first + iota(panel.shape, 1)
    local = ids - tile * TILE
    own = (local >= 0) & (local < TILE)
    beside = ids - other * TILE
    gone = (beside >= 0) & (beside < TILE)
    panel = jnp.where(own, jnp.where(local == iota(panel.shape, 0), -1.0, 0.0), panel)
    return jnp.where(gone, 0.0, panel)


def main_kernel(
    a_ref, shift, piv,
    schur, lower,
    raw,     x_buf, r_buf, p0c_buf, n_buf, cand, pcand, cm, pm, rs1, rs2, acc, y, hpre, p2, p2sum, p3, pv, gr, gsum, gp, g, u, mparts, pparts,
    sem_p1, sem_c1, sem_h1, s_p2, r_p2, s_p3, r_p3, s_p4, r_p4, s_p5, r_p5,
    s_g1, r_g1, s_g2, r_g2, s_g3, r_g3, s_g4, r_g4,
    s_rs, r_rs, s_h, r_h, s_agr, s_agl, r_ag, s_ahr, s_ahl, r_ah,
    s_sib, r_sib, s_sibh, r_sibh, s_xa, s_xb, r_x, s_raw, r_raw, s_sw, r_sw,
):
    d, r, c = lax.axis_index("dir"), lax.axis_index("row"), lax.axis_index("col")
    s, z_hi = r % 2, r // 2
    z = 2 * z_hi + d
    cx, cy = c % 4, c // 4
    own = s == d
    other = s != d

    def at(zz, cc):
        return (zz % 2, 2 * (zz // 2) + s, cc)

    sibling = (d, r + 1 - 2 * s, c)
    partner = (1 - d, r, c)

    def copy(src, dst, send, recv, device):
        return pltpu.make_async_remote_copy(
            src_ref=src, dst_ref=dst, send_sem=send, recv_sem=recv, device_id=device, device_id_type=MESH
        )

    def span(first, count):
        return pl.ds(pl.multiple_of(first, 8), count)

    barrier = pltpu.get_barrier_semaphore()
    pl.semaphore_signal(barrier, inc=1, device_id=sibling, device_id_type=MESH)
    for o in range(1, 8):
        pl.semaphore_signal(barrier, inc=1, device_id=at((z + o) % 8, c), device_id_type=MESH)
    for o in range(1, 16):
        pl.semaphore_signal(barrier, inc=1, device_id=at(z, (c + o) % 16), device_id_type=MESH)

    tiles = (piv[d, 0], piv[d, 1])
    col_ids = c * 768 + iota((TILE, 768), 1)
    for k in range(2):
        named = jnp.full((TILE, 768), tiles[k], jnp.int32)
        block = jnp.zeros((TILE, 768), F32)
        for j in range(6):
            block = jnp.where(named == 6 * r + j, a_ref[0, TILE * j : TILE * j + TILE, :], block)
        ids = tiles[k] * TILE + iota((TILE, 768), 0)
        here = (ids == col_ids) & (ids >= r * 1536) & (ids < r * 1536 + 1536)
        cand[k] = block + jnp.where(here, shift[...], 0.0)
    lead = a_ref[0, 0:TILE, :] + jnp.where(iota((TILE, 768), 0) == col_ids, shift[...], 0.0)
    gone = (col_ids // TILE == tiles[0]) | (col_ids // TILE == tiles[1]) | (iota((TILE, 768), 0) + r * 1536 >= 1536)
    cand[2] = jnp.where(gone, 0.0, lead)
    for k in range(2):
        named = jnp.full((2 * TILE, TILE), tiles[k], jnp.int32)
        block = jnp.zeros((2 * TILE, TILE), F32)
        for j in range(3):
            part = cand[0:2, :, TILE * j : TILE * j + TILE].reshape(2 * TILE, TILE)
            block = jnp.where(named == 3 * c + j, part, block)
        pcand[:, TILE * k : TILE * k + TILE] = block
    pl.semaphore_wait(barrier, 23)

    def merge_p():
        return copy(pcand, pm, sem_p1.at[0], sem_p1.at[1], sibling)

    def merge_c():
        return copy(cand.at[pl.ds(0, 2)], cm.at[pl.ds(0, 2)], sem_c1.at[0], sem_c1.at[1], sibling)

    def h_first():
        return copy(cand.at[2], hpre, sem_h1.at[0], sem_h1.at[1], partner)

    def p2_copy(o, cc, slot):
        return copy(pm.at[span(32 * cc, 32), :], p2.at[slot], s_p2.at[o - 1], r_p2.at[slot], at(z, cc))

    def rs_first(way, layer):
        q = (layer + 2) % 4
        k = (1 - way) // 2
        return copy(
            cm.at[pl.ds(0, 2), span(64 * q + 32 * k, 32), :], rs1.at[k], s_rs.at[k], r_rs.at[k],
            at(2 * ((layer + way + 4) % 4) + d, c),
        )

    def rs_second(way, layer):
        q = (layer + way + 4) % 4
        k = (1 - way) // 2
        return copy(
            acc.at[k], rs2.at[k], s_rs.at[2 + k], r_rs.at[2 + k], at(2 * q + d, c)
        )

    def h_copy(q):
        rows = span(64 * q, 64)
        return copy(cm.at[2, rows, :], y.at[2, rows, :], s_h.at[q - 1], r_h.at[0], at(2 * q + d, c))

    def p3_copy(o, q, slot):
        return copy(p2sum.at[span(8 * q, 8), :], p3.at[slot], s_p3.at[o - 1], r_p3.at[slot], at(2 * q + d, c))

    def p4_copy(o, zz, slot):
        rows = span(32 * c + 8 * slot, 8)
        return copy(pv.at[rows, :], pv.at[rows, :], s_p4.at[o - 1], r_p4.at[slot], at(zz, c))

    def p5_copy(o, cc, slot):
        rows = span(32 * slot, 32)
        return copy(pv.at[rows, :], pv.at[rows, :], s_p5.at[o - 1], r_p5.at[slot], at(z, cc))

    def g1_copy(o, q, slot):
        return copy(
            cm.at[:, span(64 * q, 64), pl.ds(0, TILE)], gr.at[slot], s_g1.at[o - 1], r_g1.at[slot], at(2 * q + d, c)
        )

    def g2_copy(cc):
        return copy(
            gsum.at[:, span(8 * cc, 8), :], gp.at[cc, :, span(8 * z_hi, 8), :], s_g2.at[cc - 1], r_g2.at[0], at(z, cc)
        )

    def g3_copy(o, zz, slot):
        block = gp.at[c, :, span(8 * slot, 8), :]
        return copy(block, block, s_g3.at[o - 1], r_g3.at[slot], at(zz, c))

    def g4_copy(o, cc, slot):
        return copy(gp.at[slot], gp.at[slot], s_g4.at[o - 1], r_g4.at[slot], at(z, cc))

    def raw_copy(k):
        return copy(
            a_ref.at[0, span((1 - d) * 768 + 128 * k, 128), :],
            raw.at[pl.ds(128 * k, 128), :], s_raw.at[k], r_raw.at[k], partner,
        )

    sends_h = (d == 1) & (r == 0)
    leads_h = (d == 0) & (r == 0)

    @pl.when(other)
    def _():
        merge_p().start()
        merge_c().start()

    @pl.when(sends_h)
    def _():
        h_first().start()

    @pl.when(s == 1)
    def _():
        y[2] = jnp.zeros((TILE, 768), F32)

    def push_g4():
        @pl.when(c < 8)
        def _():
            for o in range(1, 16):
                g4_copy(o, (c + o) % 16, c).start()

    @pl.when(own)
    def _():
        merge_p().wait_recv()
        pm[...] = pm[...] + pcand[...]
        for o in range(1, 16):
            p2_copy(o, (c + o) % 16, c).start()
        merge_c().wait_recv()
        cm[0:2] = cm[0:2] + cand[0:2]

        @pl.when(leads_h)
        def _():
            h_first().wait_recv()
            cm[2] = cand[2] + hpre[...]

        @pl.when(r != d)
        def _():
            cm[2] = jnp.zeros((TILE, 768), F32)

        @pl.when((r == d) & (d == 1))
        def _():
            cm[2] = jnp.zeros((TILE, 768), F32)

        total = pm[span(32 * c, 32), :]
        for o in range(1, 16):
            cc = (c + o) % 16
            p2_copy(o, cc, cc).wait_recv()
            total = total + p2[cc]
        p2sum[...] = total
        for o in range(1, 4):
            p3_copy(o, (z_hi + o) % 4, z_hi).start()

        total = p2sum[span(8 * z_hi, 8), :]
        for o in range(1, 4):
            q = (z_hi + o) % 4
            p3_copy(o, q, q).wait_recv()
            total = total + p3[q]
        pv[span(32 * c + 8 * z_hi, 8), :] = total
        for o in range(1, 8):
            p4_copy(o, (z + o) % 8, z_hi).start()

        @pl.when(c == 0)
        def _():
            for o in range(1, 4):
                g1_copy(o, (z_hi + o) % 4, z_hi).start()

        for way in (1, -1):
            rs_first(way, z_hi).start()

        @pl.when(leads_h)
        def _():
            for q in range(1, 4):
                h_copy(q).start()
            y[2, 0:64, :] = cm[2, 0:64, :]

        for o in range(1, 4):
            q = (z_hi + o) % 4
            p4_copy(o, z, q).wait_recv()

    @pl.when(other)
    def _():
        for q in range(4):
            p4_copy(1, z, q).wait_recv()

    for o in range(1, 16):
        p5_copy(o, (c + o) % 16, c).start()

    @pl.when(own)
    def _():
        for way in (1, -1):
            k = (1 - way) // 2
            rs_first(way, z_hi).wait_recv()
            acc[k] = cm[0:2, span(64 * ((z_hi + way + 4) % 4), 64), :]
            acc[k, :, 32 * k : 32 * k + 32, :] = acc[k, :, 32 * k : 32 * k + 32, :] + rs1[k]
            rs_second(way, z_hi).start()

    def order(e, k):
        delta = jnp.where(
            e == d,
            jnp.where(k == 0, 0, jnp.where(k == 1, 2, jnp.where(k == 2, 6, 4))),
            jnp.where(k == 0, 1, jnp.where(k == 1, 7, jnp.where(k == 2, 3, 5))),
        )
        return (((z - (1 - 2 * e) * delta + 16) % 8 - e + 8) // 2) % 4

    class Ring:
        def __init__(self, k, step):
            q = order(s, k)
            rows = span(64 * q, 64)
            right = step == 1
            to = at((z + step * (1 - 2 * s) + 8) % 8, c)
            block = y.at[pl.ds(0, 2), rows, :]
            self.main = copy(block, block, (s_agr if right else s_agl).at[q], r_ag.at[q], to)
            block = y.at[2, rows, :]
            self.lead = copy(block, block, (s_ahr if right else s_ahl).at[q], r_ah.at[q], to)

        def both(self, name):
            getattr(self.main, name)()

            @pl.when(s == 0)
            def _():
                getattr(self.lead, name)()

    def arrive(k):
        Ring(k, 1).both("wait_recv")

    def stage(k):
        if k == 0 or k == 2:
            @pl.when(other)
            def _():
                arrive(k)
                Ring(k, 1).both("start")
                arrive(k + 1)
                if k == 0:
                    Ring(k + 1, -1).both("start")
        elif k == 1:
            @pl.when(own)
            def _():
                arrive(1)
                Ring(1, 1).both("start")
                arrive(2)
                Ring(2, -1).both("start")
        else:
            @pl.when(own)
            def _():
                arrive(3)

    k_own = 2 * r + d
    k_sib = 2 * (r + 1 - 2 * s) + d
    xs, ys = k_own % 4, k_own // 4

    def sib_panels(e, k):
        rows = span(64 * order(e, k), 64)
        return copy(
            y.at[pl.ds(0, 2), rows, :], x_buf.at[pl.ds(2 * e, 2), rows, :], s_sib.at[k], r_sib.at[k], sibling
        )

    def sib_h(k):
        rows = span(64 * order(0, k), 64)
        return copy(y.at[2, rows, :], x_buf.at[4, rows, :], s_sibh.at[k], r_sibh.at[k], sibling)

    def to_root(k):
        @pl.when(c == k_sib)
        def _():
            sib_panels(s, k).start()

            @pl.when(s == 0)
            def _():
                sib_h(k).start()

        @pl.when(c == k_own)
        def _():
            rows = span(64 * order(s, k), 64)
            x_buf[pl.ds(2 * s, 2), rows, :] = y[0:2, rows, :]

            @pl.when(s == 0)
            def _():
                x_buf[4, rows, :] = y[2, rows, :]

            sib_panels(1 - s, k).wait_recv()

            @pl.when(s == 1)
            def _():
                sib_h(k).wait_recv()

    def tree(t, slot):
        way = 1 if t % 2 == 0 else -1
        dx = (way * (cx - xs) + 4) % 4
        dy = (way * (cy - ys) + 4) % 4
        depth = dx + dy
        if t < 2:
            to_x = (dy == 0) & (dx < 3)
            to_y = dy < 3
        else:
            to_x = (dy >= 1) & (dx < 3)
            to_y = ((dx == 0) & (dy < 3)) | ((dx >= 1) & (dy == 3))
            depth = depth + jnp.where((dy == 0) & (dx >= 1), 4, 0)
        p = slot - 3 * depth
        valid = (p >= 0) & (p < 20)
        p = jnp.where(valid, p, 0)
        tile = p % 5
        rows = span(64 * order(jnp.where(tile == 4, 0, tile // 2), p // 5) + 16 * t, 16)
        block = x_buf.at[tile, rows, :]
        next_x = at(z, 4 * cy + (cx + way + 4) % 4)
        next_y = at(z, 4 * ((cy + way + 4) % 4) + cx)
        copy_x = copy(block, block, s_xa.at[t, p], r_x.at[t, p], next_x)
        copy_y = copy(block, block, s_xb.at[t, p], r_x.at[t, p], next_y)
        return valid, depth, to_x, to_y, copy_x, copy_y

    def x_slot(slot):
        for t in range(4):
            valid, depth, to_x, to_y, copy_x, copy_y = tree(t, slot)

            @pl.when(valid & (depth > 0))
            def _():
                copy_x.wait_recv()

            @pl.when(valid & to_x)
            def _():
                copy_x.start()

            @pl.when(valid & to_y)
            def _():
                copy_y.start()

    def x_end(slot):
        for t in range(4):
            valid, _, to_x, to_y, copy_x, copy_y = tree(t, slot)

            @pl.when(valid & to_x)
            def _():
                copy_x.wait_send()

            @pl.when(valid & to_y)
            def _():
                copy_y.wait_send()

    for o in range(1, 16):
        cc = (c + o) % 16
        p5_copy(o, cc, cc).wait_recv()
    for o in range(1, 16):
        p5_copy(o, (c + o) % 16, c).wait_send()

    @pl.when(own)
    def _():
        for o in range(1, 8):
            p4_copy(o, (z + o) % 8, z_hi).wait_send()

    def end_reduce():
        @pl.when(own)
        def _():
            rows = span(64 * z_hi, 64)
            total = cm[0:2, rows, :]
            for way in (1, -1):
                rs_second(way, z_hi).wait_recv()
                total = total + rs2[(1 - way) // 2]
            y[0:2, rows, :] = total

            @pl.when((d == 0) & (r != 0))
            def _():
                h_copy(z_hi).wait_recv()

            Ring(0, 1).both("start")
            Ring(0, -1).both("start")

    @pl.when(own)
    def _():
        @pl.when(c == 0)
        def _():
            total = cm[:, span(64 * z_hi, 64), 0:TILE]
            for o in range(1, 4):
                q = (z_hi + o) % 4
                g1_copy(o, q, q).wait_recv()
                total = total + gr[q]
            gsum[...] = total
            for cc in range(1, 8):
                g2_copy(cc).start()
            gp[0, :, span(8 * z_hi, 8), :] = total[:, 0:8]

    def between(p, i):
        @pl.when((p == 0) & (i == 2) & own)
        def _():
            @pl.when((c > 0) & (c < 8))
            def _():
                g2_copy(c).wait_recv()

            @pl.when(c < 8)
            def _():
                for o in range(1, 8):
                    g3_copy(o, (z + o) % 8, z_hi).start()

        x_slot(5 * (p - 2) + i)

    def outer(p, carry):
        sweep_step(pv, p, lambda i: between(p, i))
        x_slot(5 * (p - 2) + 4)

        @pl.when(p == 0)
        def _():
            end_reduce()

        for k in range(3):
            @pl.when(p == k + 1)
            def _():
                stage(k)

        @pl.when(p >= 1)
        def _():
            to_root(p - 1)

        @pl.when(p == 1)
        def _():
            @pl.when(own & (c < 8))
            def _():
                for o in range(1, 4):
                    q = (z_hi + o) % 4
                    g3_copy(o, z, q).wait_recv()

            @pl.when(other & (c < 8))
            def _():
                for q in range(4):
                    g3_copy(1, z, q).wait_recv()

            push_g4()

        return carry

    lax.fori_loop(0, 4, outer, 0)
    x_slot(10)

    for o in range(1, 16):
        cc = (c + o) % 16

        @pl.when(cc < 8)
        def _():
            g4_copy(o, cc, jnp.where(cc < 8, cc, 0)).wait_recv()

    for k in range(3):
        for q in range(4):
            for cc in range(8):
                g[k, 64 * q + 8 * cc : 64 * q + 8 * cc + 8, :] = gp[cc, k, 8 * q : 8 * q + 8, :]

    x_slot(11)
    gq = g[0:2].reshape(512, TILE)
    us = -dot6(pv[...], gq, ROW_BY_COL)
    u[s] = us
    mparts[s] = g[2] - dot6(gq, us, COL_BY_COL)

    def swap(k, ref, e):
        return copy(ref.at[e], ref.at[e], s_sw.at[k], r_sw.at[k], sibling)

    def swap_r(e):
        return copy(r_buf.at[pl.ds(2 * e, 2)], r_buf.at[pl.ds(2 * e, 2)], s_sw.at[2], r_sw.at[2], sibling)

    swap(1, mparts, s).start()
    swap(0, u, s).start()
    stage(3)
    for k in range(6):
        raw_copy(k).start()
    to_root(3)
    x_slot(12)
    x_slot(13)

    t0, t1 = piv[s, 0], piv[s, 1]

    def r_step(k, carry):
        cols = pl.ds(pl.multiple_of(k * 256, 256), 256)
        first = c * 768 + k * 256
        ya = modified(y[0, :, cols], t0, t1, first)
        yb = modified(y[1, :, cols], t1, t0, first)
        rk = -dot6(pv[...], jnp.concatenate([ya, yb], axis=0), ROW_BY_COL)
        r_buf[2 * s, :, cols] = rk[:TILE]
        r_buf[2 * s + 1, :, cols] = rk[TILE:]
        pparts[s, :, cols] = y[2, :, cols] - dot6(g[0:2].reshape(512, TILE), rk, COL_BY_COL)
        x_slot(14 + k)
        return carry

    lax.fori_loop(0, 3, r_step, 0)
    swap_r(s).start()
    swap(3, pparts, s).start()

    swap(1, mparts, 1 - s).wait_recv()
    n_buf[...] = mparts[0] + mparts[1]

    def outer_lead(p, carry):
        def three_slots(i):
            for k in range(3):
                x_slot(17 + 12 * p + 3 * i + k)

        sweep_step(n_buf, p, three_slots)
        return carry

    lax.fori_loop(0, 2, outer_lead, 0)
    swap(0, u, 1 - s).wait_recv()

    swap_r(1 - s).wait_recv()
    swap(3, pparts, 1 - s).wait_recv()
    p0c_buf[...] = pparts[0] + pparts[1]

    for k in range(6):
        raw_copy(k).wait()

    def zeroed(block, ids, e):
        ta, tb = piv[e, 0], piv[e, 1]
        block = block + jnp.where(ids == col_ids, shift[...], 0.0)
        row_tile, col_tile = ids // TILE, col_ids // TILE
        hit = (row_tile == ta) | (row_tile == tb) | (col_tile == ta) | (col_tile == tb)
        return jnp.where(hit, 0.0, block)

    def last_step(k, carry):
        cols = pl.ds(pl.multiple_of(k * 256, 256), 256)
        rows = span(k * 256, 256)
        first = k_own * 768 + k * 256
        lead = x_buf[4, :, cols]
        ids = first + iota((TILE, 768), 0)
        mine = a_ref[0, span(d * 768 + k * 256, 256), :]
        total = zeroed(mine, ids, d) + zeroed(raw[rows, :], ids, 1 - d)
        for e in range(2):
            ta, tb = piv[e, 0], piv[e, 1]
            xa = modified(x_buf[2 * e, :, cols], ta, tb, first)
            xb = modified(x_buf[2 * e + 1, :, cols], tb, ta, first)
            x = jnp.concatenate([xa, xb], axis=0)
            lead = lead - dot6(u[e], x, COL_BY_COL)
            total = total - dot3(x, r_buf[2 * e : 2 * e + 2].reshape(512, 768), COL_BY_COL)
        low = -dot6(lead, n_buf[...], COL_BY_COL)
        lower[0, 0, rows, :] = low
        keep = (ids < TILE) | (col_ids < TILE)
        schur[0, 0, rows, :] = total - jnp.where(keep, 0.0, dot3(low, p0c_buf[...], ROW_BY_COL))
        return carry

    lax.fori_loop(0, 3, last_step, 0)

    @pl.when(other)
    def _():
        merge_p().wait_send()
        merge_c().wait_send()
        Ring(0, 1).both("wait_send")
        Ring(1, -1).both("wait_send")
        Ring(2, 1).both("wait_send")

    @pl.when(sends_h)
    def _():
        h_first().wait_send()

    @pl.when(own)
    def _():
        for o in range(1, 16):
            p2_copy(o, (c + o) % 16, c).wait_send()
        for way in (1, -1):
            rs_first(way, z_hi).wait_send()
            rs_second(way, z_hi).wait_send()
        for o in range(1, 4):
            p3_copy(o, (z_hi + o) % 4, z_hi).wait_send()

        @pl.when(leads_h)
        def _():
            for q in range(1, 4):
                h_copy(q).wait_send()

        @pl.when(c == 0)
        def _():
            for o in range(1, 4):
                g1_copy(o, (z_hi + o) % 4, z_hi).wait_send()
            for cc in range(1, 8):
                g2_copy(cc).wait_send()

        @pl.when(c < 8)
        def _():
            for o in range(1, 8):
                g3_copy(o, (z + o) % 8, z_hi).wait_send()

        Ring(0, 1).both("wait_send")
        Ring(0, -1).both("wait_send")
        Ring(1, 1).both("wait_send")
        Ring(2, -1).both("wait_send")

    @pl.when(c < 8)
    def _():
        for o in range(1, 16):
            g4_copy(o, (c + o) % 16, c).wait_send()

    @pl.when(c == k_sib)
    def _():
        for k in range(4):
            sib_panels(s, k).wait_send()

            @pl.when(s == 0)
            def _():
                sib_h(k).wait_send()

    def x_last(slot, carry):
        x_end(slot)
        return carry

    lax.fori_loop(0, 41, x_last, 0)
    swap(0, u, s).wait_send()
    swap(1, mparts, s).wait_send()
    swap_r(s).wait_send()
    swap(3, pparts, s).wait_send()


def run_main(prior, shift, pivots):
    vmem = pl.BlockSpec(memory_space=pltpu.VMEM)
    dma = pltpu.SemaphoreType.DMA
    return pl.pallas_call(
        main_kernel,
        out_shape=(
            jax.ShapeDtypeStruct((1, 1, 768, 768), F32),
            jax.ShapeDtypeStruct((1, 1, 768, TILE), F32),
        ),
        in_specs=[vmem, vmem, pl.BlockSpec(memory_space=pltpu.SMEM)],
        out_specs=(vmem, vmem),
        scratch_shapes=[
            pltpu.VMEM((768, 768), F32),
            pltpu.VMEM((5, 256, 768), F32),
            pltpu.VMEM((4, 256, 768), F32),
            pltpu.VMEM((256, 768), F32),
            pltpu.VMEM((256, 256), F32),
            pltpu.VMEM((3, 256, 768), F32),
            pltpu.VMEM((512, 512), F32),
            pltpu.VMEM((3, 256, 768), F32),
            pltpu.VMEM((512, 512), F32),
            pltpu.VMEM((2, 2, 32, 768), F32),
            pltpu.VMEM((2, 2, 64, 768), F32),
            pltpu.VMEM((2, 2, 64, 768), F32),
            pltpu.VMEM((3, 256, 768), F32),
            pltpu.VMEM((256, 768), F32),
            pltpu.VMEM((16, 32, 512), F32),
            pltpu.VMEM((32, 512), F32),
            pltpu.VMEM((4, 8, 512), F32),
            pltpu.VMEM((512, 512), F32),
            pltpu.VMEM((4, 3, 64, 256), F32),
            pltpu.VMEM((3, 64, 256), F32),
            pltpu.VMEM((8, 3, 32, 256), F32),
            pltpu.VMEM((3, 256, 256), F32),
            pltpu.VMEM((2, 512, 256), F32),
            pltpu.VMEM((2, 256, 256), F32),
            pltpu.VMEM((2, 256, 768), F32),
            dma((2,)), dma((2,)), dma((2,)),
            dma((15,)), dma((16,)), dma((3,)), dma((4,)), dma((7,)), dma((4,)), dma((15,)), dma((16,)),
            dma((3,)), dma((4,)), dma((7,)), dma((1,)), dma((7,)), dma((4,)), dma((15,)), dma((8,)),
            dma((4,)), dma((4,)), dma((3,)), dma((1,)),
            dma((4,)), dma((4,)), dma((4,)), dma((4,)), dma((4,)), dma((4,)),
            dma((4,)), dma((4,)), dma((4,)), dma((4,)),
            dma((4, 20)), dma((4, 20)), dma((4, 20)),
            dma((6,)), dma((6,)), dma((4,)), dma((4,)),
        ],
        compiler_params=pltpu.CompilerParams(
            collective_id=0, has_side_effects=True, vmem_limit_bytes=56 * 1024 * 1024
        ),
    )(prior, shift, pivots)


def shifts(quantum):
    quantum = quantum.astype(F32)
    return (
        0.025 * quantum[:, 0] * (quantum[:, 0] + 1.0)
        + 0.01 * quantum[:, 1] * quantum[:, 1]
        + 0.01 * quantum[:, 2] * (quantum[:, 2] + 1.0)
        + 0.005 * quantum[:, 3] * (quantum[:, 3] + 1.0)
    )


def per_device(prior_y, labels, pivots):
    first = lax.axis_index("col") * 768
    shift = shifts(lax.dynamic_slice_in_dim(labels, first, 768, 0))[None, :]
    return run_main(prior_y, shift, pivots)


def solution(mesh):
    placed = (P("dir", "row", "col"), P(), P())
    return jax.shard_map(
        per_device,
        mesh=mesh,
        in_specs=placed,
        out_specs=(P("row", "dir", None, "col"), P("row", "dir", None, None)),
        check_vma=False,
    )
```
